32 devices in a mesh: dom: 4 (over y, x), grp: 8 (over z, core).
Axes of the slice: x: 2, y: 2, z: 4, core: 2. Of those that a mesh axis runs over, the one named last changes fastest.
Arguments:
- features: bfloat16 [8192, 256], P(('dom', 'grp')), may hold values from -6 to 6
- adjacency: bfloat16 [512, 128, 128], P(('dom', 'grp')), may hold values from -0.1875 to 0.1875
- src_tile: int32 [512], P(('dom', 'grp')), may hold values from 0 to 1
- dst_peer: int32 [512, 1], P(('dom', 'grp')), may hold values from 0 to 3; in each aligned block of 16 rows (0 to 15, 16 to 31, ...) at most 8 rows name the same one
- dst_tile: int32 [512], P(('dom', 'grp')), may hold values from 0 to 1
- w_self: bfloat16 [256, 256], replicated, may hold values from -0.375 to 0.375
- w_neigh: bfloat16 [256, 256], replicated, may hold values from -0.375 to 0.375
- out_grad: bfloat16 [8192, 256], P(('dom', 'grp')), may hold values from -6 to 6
Outputs:
- output: bfloat16 [8192, 256], P(('dom', 'grp'))
- feat_grad: bfloat16 [8192, 256], P(('dom', 'grp'))
- weight_grads: float32 [2, 256, 256], replicated
The draws below stay inside these ranges and needn't reach their ends.
Inputs may be any that keep to these rules, and one draw needn't show every extreme that they name: `dst_peer`: among the 16 blocks of one device no partition is named more than 8 times, a bound that some block reaches.
All inputs are finite; a program needn't handle non-finite values.
Results may differ from the reference program's by a relative error of at most 0.015.
Values may be sent and summed in bfloat16 or wider, within the bound.
A program may use at most 64 MiB of HBM per device.

```python
import math
import jax
import jax.numpy as jnp
import numpy as np
from jax import lax

F = 256
TILE = 128
TILES_DEV = 16
NT = 2
CAP = 8
NODES = 8192
TILES = 512
N_DOM = 4
N_GRP = 8
DEVICES = 32


def touch_ends(values, rng, low, high):
    place = [jax.random.randint(jax.random.fold_in(rng, axis), (), 0, length) for axis, length in enumerate(values.shape)]
    main_axis = values.shape.index(max(values.shape))
    beside = place[:main_axis] + [(place[main_axis] + 1) % values.shape[main_axis]] + place[main_axis + 1:]
    return values.at[tuple(place)].set(low).at[tuple(beside)].set(high)


def level_of(own_key, dims, pieces, least, high):
    def one(dim, blocks):
        heights = jax.random.uniform(jax.random.fold_in(jax.random.fold_in(own_key, 6), dim), (blocks,), jnp.float32, least / len(pieces), high / len(pieces))
        return jnp.repeat(jnp.exp(heights), dims[dim] // blocks).reshape((-1,) + (1,) * (len(dims) - dim - 1))

    gain = one(*pieces[0])
    for cut in pieces[1:]:
        gain = gain * one(*cut)
    return gain


def routed_block(key, own, number, rows, count, top, limit, slope):
    order = jax.random.permutation(key, count)
    crowded, ordinary = load_shares(count, rows * top, limit, slope, True), load_shares(count, rows * top, limit, slope, False)
    places = jnp.arange(count)

    def named(tallies, turn):
        used = int((tallies > 0).sum())
        fixed = max(1, used // 4)
        moved = fixed + (places - fixed + turn * (used - fixed)) % max(1, count - fixed)
        return jnp.zeros((count,), jnp.int32).at[order[jnp.where(places < fixed, places, moved)]].set(jnp.asarray(tallies, jnp.int32))

    tallies = jnp.where(number % 4 == 0, named(crowded, number // 4), named(ordinary, number - number // 4 - 1))
    mixed = jax.random.permutation(jax.random.fold_in(own, 3), count)
    source_of, receiver = mixed[0:count // 2 * 2:2], mixed[1:count // 2 * 2:2]
    margin = jnp.minimum(tallies[source_of] - 1, limit - tallies[receiver]) // 2
    margin = jnp.where((source_of == order[0]) | (receiver == order[0]) | (tallies[receiver] == 0), 0, jnp.maximum(margin, 0))
    moved = jax.random.randint(jax.random.fold_in(own, 4), (count // 2,), 0, 1 << 20) % (margin + 1)
    tallies = tallies.at[source_of].add(-moved).at[receiver].add(moved)
    members = jnp.searchsorted(jnp.cumsum(tallies), jnp.arange(rows * top), side="right").astype(jnp.int32)
    table = members.reshape(top, rows).T
    table = table[jax.random.permutation(jax.random.fold_in(own, 1), rows)]
    turn = jax.random.randint(jax.random.fold_in(own, 2), (rows, 1), 0, top)
    return jnp.take_along_axis(table, (jnp.arange(top)[None, :] + turn) % top, axis=1)


def load_shares(amount, total, bound, skew, full):
    weights = [(1 << 20) // math.isqrt(grade ** skew) + 1 for grade in range(1, amount + 1)]
    largest = bound if full else min(bound, max(-(-total // amount), total * weights[0] // sum(weights)))
    least = 1 if total - largest >= amount - 1 else 0
    given, rest = [largest] + [least] * (amount - 1), total - largest - least * (amount - 1)
    while rest > 0:
        candidates = [i for i in range(1, amount) if given[i] < largest] or [i for i in range(1, amount) if given[i] < bound]
        mass, remaining = sum([weights[i] for i in candidates]), rest
        for i in candidates:
            more = min(bound - given[i], max(1, remaining * weights[i] // mass), rest)
            given[i] = given[i] + more
            rest = rest - more
    return np.array(given)


def centred(own_key, extent, scale, limit, pieces=(), held_as=jnp.bfloat16):
    factor_of = level_of(own_key, extent, pieces, -0.22, 0.18) if pieces else 1.0
    entries = jax.random.normal(own_key, extent, jnp.float32) * scale * factor_of
    return jnp.minimum(jnp.maximum(entries, -limit), limit).astype(held_as)


def setup_inputs(seed: int = 0) -> dict:
    splits = jax.random.split(jax.random.key(seed), 9)
    features = centred(splits[0], (NODES, F), 1.0, 6.0, ((0, 32),))
    adjacency = centred(splits[1], (TILES, TILE, TILE), (TILE * TILES_DEV // NT) ** -0.5, 0.1875, ((0, 32),))
    src_tile = touch_ends(jax.random.randint(splits[2], (TILES,), 0, NT), jax.random.fold_in(splits[2], 1), 0, NT - 1).astype(jnp.int32)
    dst_peer_keys = jax.random.split(jax.random.fold_in(splits[3], 1), TILES // TILES_DEV)
    dst_peer_turns = jax.random.permutation(jax.random.fold_in(splits[3], 3), TILES // TILES_DEV)
    dst_peer = jax.vmap(lambda own, number: routed_block(jax.random.fold_in(splits[3], 2), own, number, TILES_DEV, N_DOM, 1, CAP, 2))(dst_peer_keys, dst_peer_turns).reshape((TILES, 1))
    dst_tile = touch_ends(jax.random.randint(splits[4], (TILES,), 0, NT), jax.random.fold_in(splits[4], 1), 0, NT - 1).astype(jnp.int32)
    w_self = centred(splits[5], (F, F), F ** -0.5, 0.375)
    w_neigh = centred(splits[6], (F, F), F ** -0.5, 0.375)
    out_grad = centred(splits[7], (NODES, F), 1.0, 6.0, ((0, 32),))
    return {"features": features, "adjacency": adjacency, "src_tile": src_tile, "dst_peer": dst_peer, "dst_tile": dst_tile, "w_self": w_self, "w_neigh": w_neigh, "out_grad": out_grad}


def reference(features, adjacency, src_tile, dst_peer, dst_tile, w_self, w_neigh, out_grad):
    n_blocks = NODES // TILE
    device = jnp.arange(DEVICES, dtype=jnp.int32)
    group = device % N_GRP
    src_index = (device[:, None] * NT + src_tile.reshape(DEVICES, TILES_DEV)).astype(jnp.int32)
    dst_index = ((dst_peer[:, 0].reshape(DEVICES, TILES_DEV) * N_GRP + group[:, None]) * NT + dst_tile.reshape(DEVICES, TILES_DEV)).astype(jnp.int32)
    tiles = adjacency.reshape(DEVICES, TILES_DEV, TILE, TILE)
    blocks = features.reshape(n_blocks, TILE, F)

    def forward_step(carry, item):
        adj, src, dst = item
        prod = jnp.einsum('tij,tjf->tif', adj.astype(jnp.float32), blocks[src].astype(jnp.float32)).astype(jnp.bfloat16)
        return (carry.at[dst].add(prod.astype(jnp.float32)), None)
    agg, _ = lax.scan(forward_step, jnp.zeros((n_blocks, TILE, F), jnp.float32), (tiles, src_index, dst_index))
    agg_low = agg.reshape(NODES, F).astype(jnp.bfloat16)
    pre = jnp.dot(features, w_self, preferred_element_type=jnp.float32) + jnp.dot(agg_low, w_neigh, preferred_element_type=jnp.float32)
    sig = jax.nn.sigmoid(pre)
    output = (pre * sig).astype(jnp.bfloat16)
    dpre = (out_grad.astype(jnp.float32) * sig * (1.0 + pre * (1.0 - sig))).astype(jnp.bfloat16)
    scale = 1.0 / math.sqrt(NODES)
    grad_self = jnp.dot(features.T, dpre, preferred_element_type=jnp.float32) * scale
    grad_neigh = jnp.dot(agg_low.T, dpre, preferred_element_type=jnp.float32) * scale
    agg_grad = jnp.dot(dpre, w_neigh.T, preferred_element_type=jnp.float32).astype(jnp.bfloat16)
    grad_blocks = agg_grad.reshape(n_blocks, TILE, F)

    def backward_step(carry, item):
        adj, src, dst = item
        back = jnp.einsum('tij,tif->tjf', adj.astype(jnp.float32), grad_blocks[dst].astype(jnp.float32))
        return (carry.at[src].add(back), None)
    spread, _ = lax.scan(backward_step, jnp.zeros((n_blocks, TILE, F), jnp.float32), (tiles, src_index, dst_index))
    feat_grad = (jnp.dot(dpre, w_self.T, preferred_element_type=jnp.float32) + spread.reshape(NODES, F)).astype(jnp.bfloat16)
    return (output, feat_grad, jnp.stack([grad_self, grad_neigh]))
```

```python
import functools
import math

import jax
import jax.numpy as jnp
from jax import lax
from jax.experimental import pallas as pl
from jax.experimental.pallas import tpu as pltpu
from jax.sharding import PartitionSpec as P

MESH = pl.DeviceIdType.MESH
BF16 = jnp.bfloat16
F32 = jnp.float32
STRIP = 32
MIN_ROWS = 16
CORES = 2


def dot(a, b, ca=1, cb=0):
    return lax.dot_general(a, b, (((ca,), (cb,)), ((), ())), preferred_element_type=F32)


def kernel(
    parts, depth, reduce_here, scale,
    src_ref, peer_ref, tile_ref, x_ref, adj_ref, ws_ref, wn_ref, og_ref,
    out_ref, fg_ref, wg_ref,
    dense, fsend, frecv, gsend, grecv, both, wsend, wsib, wsum, wslots, wfull,
    fs_sem, fr_sem, gs_sem, gr_sem, sib_s, sib_r, rs_s, rs_r, ag_s, ag_r,
):
    dom = lax.axis_index("dom")
    grp = lax.axis_index("grp")
    count, tile = adj_ref.shape[0], adj_ref.shape[1]
    nodes, width = x_ref.shape
    nt = nodes // tile
    core = lax.rem(grp, CORES)
    layer = grp // CORES
    chips = parts * depth
    here = dom * depth + layer
    sibling = (dom, layer * CORES + (1 - core))

    def peer_at(k):
        return (lax.rem(dom + k, parts), grp)

    def chip_at(k):
        index = lax.rem(here + k, chips)
        return index, (index // depth, lax.rem(index, depth) * CORES + core)

    barrier = pltpu.get_barrier_semaphore()
    if reduce_here:
        for k in range(1, chips):
            pl.semaphore_signal(barrier, inc=1, device_id=chip_at(k)[1], device_id_type=MESH)
        pl.semaphore_signal(barrier, inc=1, device_id=sibling, device_id_type=MESH)
        greeted = chips
    else:
        for k in range(1, parts):
            pl.semaphore_signal(barrier, inc=1, device_id=peer_at(k), device_id_type=MESH)
        greeted = parts - 1

    codes = [(peer_ref[t] * nt + tile_ref[t]) * nt + src_ref[t] for t in range(count)]

    def build(k):
        base = lax.rem(dom + k, parts) * (nt * nt)
        marks = [
            [jnp.where(code - base == c, 1.0, 0.0).astype(F32) for c in range(nt * nt)]
            for code in codes
        ]

        def strip(i, carry):
            start = pl.multiple_of(i * STRIP, STRIP)
            sums = [jnp.zeros((STRIP, tile), F32) for _ in range(nt * nt)]
            for t in range(count):
                block = adj_ref[t, pl.ds(start, STRIP), :].astype(F32)
                for c in range(nt * nt):
                    sums[c] = sums[c] + marks[t][c] * block
            for c in range(nt * nt):
                rows = pl.ds((c // nt) * tile + start, STRIP)
                cols = pl.ds((c % nt) * tile, tile)
                dense[k, rows, cols] = sums[c].astype(BF16)
            return carry

        lax.fori_loop(0, tile // STRIP, strip, 0)

    def forward_copy(k):
        return pltpu.make_async_remote_copy(
            src_ref=fsend.at[k], dst_ref=frecv.at[k], send_sem=fs_sem.at[k], recv_sem=fr_sem.at[k],
            device_id=peer_at(k), device_id_type=MESH,
        )

    def gather_copy(k):
        return pltpu.make_async_remote_copy(
            src_ref=gsend, dst_ref=grecv.at[k], send_sem=gs_sem.at[k], recv_sem=gr_sem.at[k],
            device_id=peer_at(k), device_id_type=MESH,
        )

    x = x_ref[...]
    for k in range(1, parts):
        build(k)
        fsend[k] = dot(dense[k], x).astype(BF16)
        if k == 1:
            pl.semaphore_wait(barrier, greeted)
        forward_copy(k).start()
    build(0)
    agg = dot(dense[0], x)
    pre_self = dot(x, ws_ref[...])
    both[0] = x
    for k in range(1, parts):
        forward_copy(k).wait_recv()
        agg = agg + frecv[k].astype(F32)
    agg_low = agg.astype(BF16)
    both[1] = agg_low
    pre = pre_self + dot(agg_low, wn_ref[...])
    sig = jax.nn.sigmoid(pre)
    dpre = (og_ref[...].astype(F32) * sig * (1.0 + pre * (1.0 - sig))).astype(BF16)

    def sibling_copy(i, src, dst):
        return pltpu.make_async_remote_copy(
            src_ref=src, dst_ref=dst, send_sem=sib_s.at[i], recv_sem=sib_r.at[i],
            device_id=sibling, device_id_type=MESH,
        )

    if reduce_here:
        halving = sibling_copy(0, wsend, wsib)
        wsend[...] = dot(both[1 - core], dpre, 0, 0).astype(BF16)
        halving.start()
    gsend[...] = dot(dpre, wn_ref[...], 1, 1).astype(BF16)
    for k in range(1, parts):
        gather_copy(k).start()
    out_ref[...] = (pre * sig).astype(BF16)

    if reduce_here:
        rows = width // chips

        def scatter_copy(k):
            index, target = chip_at(k)
            start = pl.multiple_of(index * rows, rows)
            return pltpu.make_async_remote_copy(
                src_ref=wsum.at[pl.ds(start, rows)], dst_ref=wslots.at[k],
                send_sem=rs_s.at[k], recv_sem=rs_r.at[k], device_id=target, device_id_type=MESH,
            )

        mine = pl.ds(pl.multiple_of(here * rows, rows), rows)

        def spread_copy(k):
            return pltpu.make_async_remote_copy(
                src_ref=wfull.at[core, mine], dst_ref=wfull.at[core, mine],
                send_sem=ag_s.at[k], recv_sem=ag_r.at[k], device_id=chip_at(k)[1], device_id_type=MESH,
            )

        own = dot(both[core], dpre, 0, 0)
        halving.wait_recv()
        wsum[...] = (own + wsib[...].astype(F32)).astype(BF16)
        for k in range(1, chips):
            scatter_copy(k).start()
    else:
        wg_ref[0] = dot(x, dpre, 0, 0)
        wg_ref[1] = dot(agg_low, dpre, 0, 0)

    grad = dot(dpre, ws_ref[...], 1, 1) + dot(dense[0], gsend[...], 0, 0)

    if reduce_here:
        total = wsum[mine, :].astype(F32)
        for k in range(1, chips):
            scatter_copy(k).wait_recv()
            total = total + wslots[k].astype(F32)
        wfull[core, mine, :] = (total * scale).astype(BF16)
        for k in range(1, chips):
            spread_copy(k).start()

    for k in range(1, parts):
        gather_copy(k).wait_recv()
        grad = grad + dot(dense[parts - k], grecv[k], 0, 0)
    fg_ref[...] = grad.astype(BF16)

    if reduce_here:
        for k in range(1, chips):
            spread_copy(k).wait_recv()
        final = sibling_copy(1, wfull.at[core], wfull.at[core])
        final.start()
        wg_ref[core] = wfull[core]
        final.wait_recv()
        wg_ref[1 - core] = wfull[1 - core]
        halving.wait_send()
        final.wait_send()
        for k in range(1, chips):
            scatter_copy(k).wait_send()
            spread_copy(k).wait_send()
    for k in range(1, parts):
        forward_copy(k).wait_send()
        gather_copy(k).wait_send()


def body(features, adjacency, src_tile, dst_peer, dst_tile, w_self, w_neigh, out_grad):
    nodes, width = features.shape
    parts, groups = lax.axis_size("dom"), lax.axis_size("grp")
    depth = groups // CORES
    chips = parts * depth
    reduce_here = width % chips == 0 and (width // chips) % MIN_ROWS == 0
    scale = 1.0 / math.sqrt(nodes * parts * groups)
    rows = width // chips if reduce_here else MIN_ROWS
    slots = chips if reduce_here else 1
    vmem = pl.BlockSpec(memory_space=pltpu.VMEM)
    smem = pl.BlockSpec(memory_space=pltpu.SMEM)
    square = (nodes, width)
    dma = pltpu.SemaphoreType.DMA
    output, feat_grad, grads = pl.pallas_call(
        functools.partial(kernel, parts, depth, reduce_here, scale),
        out_shape=(
            jax.ShapeDtypeStruct(square, BF16),
            jax.ShapeDtypeStruct(square, BF16),
            jax.ShapeDtypeStruct((2, width, width), BF16 if reduce_here else F32),
        ),
        in_specs=[smem] * 3 + [vmem] * 5,
        out_specs=(vmem, vmem, vmem),
        scratch_shapes=[
            pltpu.VMEM((parts, nodes, nodes), BF16),
            pltpu.VMEM((parts,) + square, BF16),
            pltpu.VMEM((parts,) + square, BF16),
            pltpu.VMEM(square, BF16),
            pltpu.VMEM((parts,) + square, BF16),
            pltpu.VMEM((2,) + square, BF16),
            pltpu.VMEM((width, width), BF16),
            pltpu.VMEM((width, width), BF16),
            pltpu.VMEM((width, width), BF16),
            pltpu.VMEM((slots, rows, width), BF16),
            pltpu.VMEM((2, width, width), BF16),
            dma((parts,)), dma((parts,)), dma((parts,)), dma((parts,)),
            dma((2,)), dma((2,)),
            dma((slots,)), dma((slots,)), dma((slots,)), dma((slots,)),
        ],
        compiler_params=pltpu.CompilerParams(
            collective_id=0, has_side_effects=True, vmem_limit_bytes=48 * 1024 * 1024
        ),
        name="sage_layer",
    )(src_tile, dst_peer[:, 0], dst_tile, features, adjacency, w_self, w_neigh, out_grad)
    if reduce_here:
        weight_grads = grads.astype(F32)
    else:
        weight_grads = lax.psum(grads, ("dom", "grp")) * scale
    return (output, feat_grad, weight_grads)


def solution(mesh):
    shard = ("dom", "grp")
    in_specs = (
        P(shard, None),
        P(shard, None, None),
        P(shard),
        P(shard, None),
        P(shard),
        P(),
        P(),
        P(shard, None),
    )
    out_specs = (P(shard, None), P(shard, None), P())
    return jax.shard_map(body, mesh=mesh, in_specs=in_specs, out_specs=out_specs, check_vma=False)
```

```python
import functools
import math

import jax
import jax.numpy as jnp
from jax import lax
from jax.experimental import pallas as pl
from jax.experimental.pallas import tpu as pltpu
from jax.sharding import PartitionSpec as P

MESH = pl.DeviceIdType.MESH
BF16 = jnp.bfloat16
F32 = jnp.float32
STRIP = 32
MIN_ROWS = 16
CORES = 2
GROUP = 4
VMEM_BYTES = 63 * 1024 * 1024


def dot(a, b, ca=1, cb=0):
    return lax.dot_general(a, b, (((ca,), (cb,)), ((), ())), preferred_element_type=F32)


def flip(index, k, size):
    total, bit = 0, 1
    while bit < size:
        digit = lax.rem(index // bit, 2)
        total = total + bit * ((1 - digit) if (k // bit) % 2 else digit)
        bit *= 2
    return total


def kernel(
    parts, depth, reduce_here, scale,
    src_hbm, peer_hbm, tile_hbm, x_hbm, adj_hbm, ws_hbm, wn_hbm, og_hbm,
    out_hbm, fg_hbm, wg_hbm,
    src_ref, peer_ref, tile_ref, x_ref, adj_ref, ws_ref, wn_ref, og_ref,
    dense, dense_t, fsend, frecv, gsend, grecv, both_t, wsend, wsib, wsum, wslots, wfull, out_ref, fg_ref, wg_ref,
    in_sem, out_sem, fs_sem, fr_sem, gs_sem, gr_sem, sib_s, sib_r, rs_s, rs_r, ag_s, ag_r,
):
    dom = lax.axis_index("dom")
    grp = lax.axis_index("grp")
    count, tile = adj_ref.shape[0], adj_ref.shape[1]
    nodes, width = x_ref.shape
    nt = nodes // tile
    core = lax.rem(grp, CORES)
    layer = grp // CORES
    chips = parts * depth
    here = dom * depth + layer
    sibling = (dom, layer * CORES + (1 - core))

    loads = [
        pltpu.make_async_copy(hbm, local, in_sem.at[i])
        for i, (hbm, local) in enumerate([
            (peer_hbm, peer_ref), (tile_hbm, tile_ref), (src_hbm, src_ref), (adj_hbm, adj_ref),
            (x_hbm, x_ref), (ws_hbm, ws_ref), (wn_hbm, wn_ref), (og_hbm, og_ref),
        ])
    ]
    for load in loads:
        load.start()

    peers = [flip(dom, k, parts) for k in range(parts)]

    def chip_at(k):
        index = flip(here, k, chips)
        return index, (index // depth, lax.rem(index, depth) * CORES + core)

    barrier = pltpu.get_barrier_semaphore()
    if reduce_here:
        chip_ids = [chip_at(k) for k in range(chips)]
        for k in range(1, chips):
            pl.semaphore_signal(barrier, inc=1, device_id=chip_ids[k][1], device_id_type=MESH)
        pl.semaphore_signal(barrier, inc=1, device_id=sibling, device_id_type=MESH)
        greeted = chips
    else:
        for k in range(1, parts):
            pl.semaphore_signal(barrier, inc=1, device_id=(peers[k], grp), device_id_type=MESH)
        greeted = parts - 1

    for load in loads[:5]:
        load.wait()
    codes = [(peer_ref[t] * nt + tile_ref[t]) * nt + src_ref[t] for t in range(count)]

    def build(k):
        base = peers[k] * (nt * nt)
        marks = [
            [jnp.where(code - base == c, 1.0, 0.0).astype(F32) for c in range(nt * nt)]
            for code in codes
        ]

        def strip(i, carry):
            start = pl.multiple_of(i * STRIP, STRIP)
            sums = [jnp.zeros((STRIP, tile), F32) for _ in range(nt * nt)]
            for t in range(count):
                block = adj_ref[t, pl.ds(start, STRIP), :].astype(F32)
                for c in range(nt * nt):
                    sums[c] = sums[c] + marks[t][c] * block
            for c in range(nt * nt):
                rows = pl.ds((c // nt) * tile + start, STRIP)
                cols = pl.ds((c % nt) * tile, tile)
                dense[k, rows, cols] = sums[c].astype(BF16)
            return carry

        lax.fori_loop(0, tile // STRIP, strip, 0)

    def forward_copy(k):
        return pltpu.make_async_remote_copy(
            src_ref=fsend.at[k], dst_ref=frecv.at[k], send_sem=fs_sem.at[k], recv_sem=fr_sem.at[k],
            device_id=(peers[k], grp), device_id_type=MESH,
        )

    def gather_copy(k):
        return pltpu.make_async_remote_copy(
            src_ref=gsend, dst_ref=grecv.at[k], send_sem=gs_sem.at[k], recv_sem=gr_sem.at[k],
            device_id=(peers[k], grp), device_id_type=MESH,
        )

    x = x_ref[...]
    order = list(range(parts - 1, 0, -1))
    for k in order:
        build(k)
        fsend[k] = dot(dense[k], x).astype(BF16)
        if k == order[0]:
            pl.semaphore_wait(barrier, greeted)
        forward_copy(k).start()
    build(0)
    for load in loads[5:]:
        load.wait()
    agg = dot(dense[0], x)
    pre_self = dot(x, ws_ref[...])
    both_t[0] = x.T
    for k in range(parts):
        dense_t[k] = dense[k].T
    for k in order:
        forward_copy(k).wait_recv()
        agg = agg + frecv[k].astype(F32)
    agg_low = agg.astype(BF16)
    both_t[1] = agg_low.T
    pre = pre_self + dot(agg_low, wn_ref[...])
    sig = jax.nn.sigmoid(pre)
    dpre = (og_ref[...].astype(F32) * sig * (1.0 + pre * (1.0 - sig))).astype(BF16)

    def sibling_copy(i, src, dst):
        return pltpu.make_async_remote_copy(
            src_ref=src, dst_ref=dst, send_sem=sib_s.at[i], recv_sem=sib_r.at[i],
            device_id=sibling, device_id_type=MESH,
        )

    if reduce_here:
        halving = sibling_copy(chips // GROUP, wsend, wsib)
        wsend[...] = dot(both_t[1 - core], dpre).astype(BF16)
        halving.start()
    gsend[...] = dot(dpre, wn_ref[...], 1, 1).astype(BF16)
    for k in order:
        gather_copy(k).start()

    if reduce_here:
        rows = width // chips

        def scatter_copy(k):
            index, target = chip_ids[k]
            start = pl.multiple_of(index * rows, rows)
            return pltpu.make_async_remote_copy(
                src_ref=wsum.at[pl.ds(start, rows)], dst_ref=wslots.at[k],
                send_sem=rs_s.at[k], recv_sem=rs_r.at[k], device_id=target, device_id_type=MESH,
            )

        mine = pl.ds(pl.multiple_of(here * rows, rows), rows)

        def spread_copy(k):
            return pltpu.make_async_remote_copy(
                src_ref=wfull.at[core, mine], dst_ref=wfull.at[core, mine],
                send_sem=ag_s.at[k], recv_sem=ag_r.at[k], device_id=chip_ids[k][1], device_id_type=MESH,
            )

        own = dot(both_t[core], dpre)
        halving.wait_recv()
        wsum[...] = (own + wsib[...].astype(F32)).astype(BF16)
        for k in range(chips - 1, 0, -1):
            scatter_copy(k).start()
    else:
        wg_ref[0] = dot(both_t[0], dpre)
        wg_ref[1] = dot(both_t[1], dpre)
        whole = pltpu.make_async_copy(wg_ref, wg_hbm, out_sem.at[2])
        whole.start()

    out_ref[...] = (pre * sig).astype(BF16)
    stores = [
        pltpu.make_async_copy(out_ref, out_hbm, out_sem.at[0]),
        pltpu.make_async_copy(fg_ref, fg_hbm, out_sem.at[1]),
    ]
    stores[0].start()
    grad = dot(dpre, ws_ref[...], 1, 1) + dot(dense_t[0], gsend[...])

    if reduce_here:
        total = wsum[mine, :].astype(F32)
        for k in range(1, chips):
            scatter_copy(k).wait_recv()
            total = total + wslots[k].astype(F32)
        wfull[core, mine, :] = (total * scale).astype(BF16)
        for k in range(chips - 1, 0, -1):
            spread_copy(k).start()

    for k in order[::-1]:
        gather_copy(k).wait_recv()
        grad = grad + dot(dense_t[k], grecv[k])
    fg_ref[...] = grad.astype(BF16)
    stores[1].start()

    if reduce_here:
        finals = []
        for j in range(chips // GROUP):
            for k in range(j * GROUP, j * GROUP + GROUP):
                if k:
                    spread_copy(k).wait_recv()
            first = flip(here // GROUP, j, chips // GROUP) * (GROUP * rows)
            piece = wfull.at[core, pl.ds(pl.multiple_of(first, GROUP * rows), GROUP * rows)]
            finals.append(sibling_copy(j, piece, piece))
            finals[-1].start()
        first_half = pltpu.make_async_copy(wg_ref.at[core], wg_hbm.at[core], out_sem.at[2])
        other_half = pltpu.make_async_copy(wg_ref.at[1 - core], wg_hbm.at[1 - core], out_sem.at[3])
        wg_ref[core] = wfull[core].astype(F32)
        first_half.start()
        for final in finals:
            final.wait_recv()
        wg_ref[1 - core] = wfull[1 - core].astype(F32)
        other_half.start()
        stores += [first_half, other_half]
        halving.wait_send()
        for final in finals:
            final.wait_send()
        for k in range(1, chips):
            scatter_copy(k).wait_send()
            spread_copy(k).wait_send()
    else:
        stores.append(whole)
    for k in order:
        forward_copy(k).wait_send()
        gather_copy(k).wait_send()
    for store in stores:
        store.wait()


def finish(out_ref, fg_ref, wg_ref, out_hbm, fg_hbm, wg_hbm, sem):
    copies = [
        pltpu.make_async_copy(wg_ref.at[0], wg_hbm.at[0], sem.at[0]),
        pltpu.make_async_copy(wg_ref.at[1], wg_hbm.at[1], sem.at[1]),
        pltpu.make_async_copy(out_ref, out_hbm, sem.at[2]),
        pltpu.make_async_copy(fg_ref, fg_hbm, sem.at[3]),
    ]
    for copy in copies:
        copy.start()
    for copy in copies:
        copy.wait()


def body(features, adjacency, src_tile, dst_peer, dst_tile, w_self, w_neigh, out_grad):
    nodes, width = features.shape
    parts, groups = lax.axis_size("dom"), lax.axis_size("grp")
    depth = groups // CORES
    chips = parts * depth
    reduce_here = width % chips == 0 and (width // chips) % MIN_ROWS == 0
    scale = 1.0 / math.sqrt(nodes * parts * groups)
    rows = width // chips if reduce_here else MIN_ROWS
    slots = chips if reduce_here else 1
    hbm = pl.BlockSpec(memory_space=pltpu.HBM)
    square = (nodes, width)
    dma = pltpu.SemaphoreType.DMA
    output, feat_grad, grads = pl.pallas_call(
        functools.partial(kernel, parts, depth, reduce_here, scale),
        out_shape=(
            jax.ShapeDtypeStruct(square, BF16),
            jax.ShapeDtypeStruct(square, BF16),
            jax.ShapeDtypeStruct((2, width, width), F32),
        ),
        in_specs=[hbm] * 8,
        out_specs=(hbm, hbm, hbm),
        scratch_shapes=[
            pltpu.SMEM(src_tile.shape, jnp.int32),
            pltpu.SMEM(src_tile.shape, jnp.int32),
            pltpu.SMEM(src_tile.shape, jnp.int32),
            pltpu.VMEM(square, BF16),
            pltpu.VMEM(adjacency.shape, BF16),
            pltpu.VMEM(w_self.shape, BF16),
            pltpu.VMEM(w_neigh.shape, BF16),
            pltpu.VMEM(square, BF16),
            pltpu.VMEM((parts, nodes, nodes), BF16),
            pltpu.VMEM((parts, nodes, nodes), BF16),
            pltpu.VMEM((parts,) + square, BF16),
            pltpu.VMEM((parts,) + square, BF16),
            pltpu.VMEM(square, BF16),
            pltpu.VMEM((parts,) + square, BF16),
            pltpu.VMEM((2, width, nodes), BF16),
            pltpu.VMEM((width, width), BF16),
            pltpu.VMEM((width, width), BF16),
            pltpu.VMEM((width, width), BF16),
            pltpu.VMEM((slots, rows, width), BF16),
            pltpu.VMEM((2, width, width), BF16),
            pltpu.VMEM(square, BF16),
            pltpu.VMEM(square, BF16),
            pltpu.VMEM((2, width, width), F32),
            dma((8,)), dma((4,)), dma((parts,)), dma((parts,)), dma((parts,)), dma((parts,)),
            dma((chips // GROUP + 1,)), dma((chips // GROUP + 1,)),
            dma((slots,)), dma((slots,)), dma((slots,)), dma((slots,)),
        ],
        compiler_params=pltpu.CompilerParams(
            collective_id=0, has_side_effects=True, vmem_limit_bytes=VMEM_BYTES
        ),
        name="sage_layer",
    )(src_tile, dst_peer[:, 0], dst_tile, features, adjacency, w_self, w_neigh, out_grad)
    if not reduce_here:
        return (output, feat_grad, lax.psum(grads, ("dom", "grp")) * scale)
    return pl.pallas_call(
        finish,
        out_shape=(
            jax.ShapeDtypeStruct(square, BF16),
            jax.ShapeDtypeStruct(square, BF16),
            jax.ShapeDtypeStruct((2, width, width), F32),
        ),
        in_specs=[hbm] * 3,
        out_specs=(hbm, hbm, hbm),
        scratch_shapes=[dma((4,))],
        compiler_params=pltpu.CompilerParams(vmem_limit_bytes=VMEM_BYTES),
        name="write_results",
    )(output, feat_grad, grads)


def solution(mesh):
    shard = ("dom", "grp")
    in_specs = (
        P(shard, None),
        P(shard, None, None),
        P(shard),
        P(shard, None),
        P(shard),
        P(),
        P(),
        P(shard, None),
    )
    out_specs = (P(shard, None), P(shard, None), P())
    return jax.shard_map(body, mesh=mesh, in_specs=in_specs, out_specs=out_specs, check_vma=False)
```

```python
import functools
import math

import jax
import jax.numpy as jnp
from jax import lax
from jax.experimental import pallas as pl
from jax.experimental.pallas import tpu as pltpu
from jax.sharding import PartitionSpec as P

MESH = pl.DeviceIdType.MESH
BF16 = jnp.bfloat16
F32 = jnp.float32
STRIP = 32
CORES = 2
VMEM_BYTES = 63 * 1024 * 1024


def dot(a, b, ca=1, cb=0):
    return lax.dot_general(a, b, (((ca,), (cb,)), ((), ())), preferred_element_type=F32)


def flip(index, k, size):
    total, bit = 0, 1
    while bit < size:
        digit = lax.rem(index // bit, 2)
        total = total + bit * ((1 - digit) if (k // bit) % 2 else digit)
        bit *= 2
    return total


def kernel(
    parts, depth, scale,
    src_hbm, peer_hbm, tile_hbm, x_hbm, adj_hbm, ws_hbm, wn_hbm, og_hbm,
    out_hbm, fg_hbm, wg_hbm,
    src_ref, peer_ref, tile_ref, x_ref, adj_ref, ws_ref, wn_ref, og_ref,
    dense, dense_t, fsend, frecv, gsend, grecv, both_t, wsend, wsib, wsum, dslots, zslots, wfull, out_ref, fg_ref, wg_ref, local_sum,
    in_sem, out_sem, fs_sem, fr_sem, gs_sem, gr_sem, sib_s, sib_r, rs_s, rs_r, z_s, z_r, ag_s, ag_r,
):
    dom = lax.axis_index("dom")
    grp = lax.axis_index("grp")
    count, tile = adj_ref.shape[0], adj_ref.shape[1]
    nodes, width = x_ref.shape
    nt = nodes // tile
    core = lax.rem(grp, CORES)
    layer = grp // CORES
    rows = width // parts
    sibling = (dom, layer * CORES + (1 - core))

    loads = [
        pltpu.make_async_copy(hbm, local, in_sem.at[i])
        for i, (hbm, local) in enumerate([
            (peer_hbm, peer_ref), (tile_hbm, tile_ref), (src_hbm, src_ref), (adj_hbm, adj_ref),
            (x_hbm, x_ref), (ws_hbm, ws_ref), (wn_hbm, wn_ref), (og_hbm, og_ref),
        ])
    ]
    for load in loads:
        load.start()

    peers = [flip(dom, k, parts) for k in range(parts)]

    layers = [(dom, flip(layer, k, depth) * CORES + core) for k in range(depth)]

    barrier = pltpu.get_barrier_semaphore()
    partners = [(peers[k], grp) for k in range(1, parts)] + layers[1:] + [sibling]
    for partner in partners:
        pl.semaphore_signal(barrier, inc=1, device_id=partner, device_id_type=MESH)

    for load in loads[:5]:
        load.wait()
    codes = [(peer_ref[t] * nt + tile_ref[t]) * nt + src_ref[t] for t in range(count)]

    def build(k):
        base = peers[k] * (nt * nt)
        marks = [
            [jnp.where(code - base == c, 1.0, 0.0).astype(F32) for c in range(nt * nt)]
            for code in codes
        ]

        def strip(i, carry):
            start = pl.multiple_of(i * STRIP, STRIP)
            sums = [jnp.zeros((STRIP, tile), F32) for _ in range(nt * nt)]
            for t in range(count):
                block = adj_ref[t, pl.ds(start, STRIP), :].astype(F32)
                for c in range(nt * nt):
                    sums[c] = sums[c] + marks[t][c] * block
            for c in range(nt * nt):
                rows = pl.ds((c // nt) * tile + start, STRIP)
                cols = pl.ds((c % nt) * tile, tile)
                dense[k, rows, cols] = sums[c].astype(BF16)
            return carry

        lax.fori_loop(0, tile // STRIP, strip, 0)

    def forward_copy(k):
        return pltpu.make_async_remote_copy(
            src_ref=fsend.at[k], dst_ref=frecv.at[k], send_sem=fs_sem.at[k], recv_sem=fr_sem.at[k],
            device_id=(peers[k], grp), device_id_type=MESH,
        )

    def gather_copy(k):
        return pltpu.make_async_remote_copy(
            src_ref=gsend, dst_ref=grecv.at[k], send_sem=gs_sem.at[k], recv_sem=gr_sem.at[k],
            device_id=(peers[k], grp), device_id_type=MESH,
        )

    x = x_ref[...]
    order = list(range(parts - 1, 0, -1))
    for k in order:
        build(k)
        fsend[k] = dot(dense[k], x).astype(BF16)
        if k == order[0]:
            pl.semaphore_wait(barrier, len(partners))
        forward_copy(k).start()
    build(0)
    for load in loads[5:]:
        load.wait()
    agg = dot(dense[0], x)
    pre_self = dot(x, ws_ref[...])
    both_t[0] = x.T
    for k in range(parts):
        dense_t[k] = dense[k].T
    for k in order:
        forward_copy(k).wait_recv()
        agg = agg + frecv[k].astype(F32)
    agg_low = agg.astype(BF16)
    both_t[1] = agg_low.T
    pre = pre_self + dot(agg_low, wn_ref[...])
    sig = jax.nn.sigmoid(pre)
    dpre = (og_ref[...].astype(F32) * sig * (1.0 + pre * (1.0 - sig))).astype(BF16)

    def sibling_copy(i, src, dst):
        return pltpu.make_async_remote_copy(
            src_ref=src, dst_ref=dst, send_sem=sib_s.at[i], recv_sem=sib_r.at[i],
            device_id=sibling, device_id_type=MESH,
        )

    halving = sibling_copy(parts, wsend, wsib)
    wsend[...] = dot(both_t[1 - core], dpre).astype(BF16)
    halving.start()
    gsend[...] = dot(dpre, wn_ref[...], 1, 1).astype(BF16)
    own = dot(both_t[core], dpre)

    def scatter_copy(k):
        start = pl.multiple_of(peers[k] * rows, rows)
        return pltpu.make_async_remote_copy(
            src_ref=wsum.at[pl.ds(start, rows)], dst_ref=dslots.at[k], send_sem=rs_s.at[k],
            recv_sem=rs_r.at[k], device_id=(peers[k], grp), device_id_type=MESH,
        )

    def layer_copy(k):
        return pltpu.make_async_remote_copy(
            src_ref=zslots.at[layer], dst_ref=zslots.at[layer], send_sem=z_s.at[k],
            recv_sem=z_r.at[k], device_id=layers[k], device_id_type=MESH,
        )

    mine = pl.ds(pl.multiple_of(dom * rows, rows), rows)

    def spread_copy(k):
        return pltpu.make_async_remote_copy(
            src_ref=wfull.at[core, mine], dst_ref=wfull.at[core, mine], send_sem=ag_s.at[k],
            recv_sem=ag_r.at[k], device_id=(peers[k], grp), device_id_type=MESH,
        )

    halving.wait_recv()
    wsum[...] = (own + wsib[...].astype(F32)).astype(BF16)
    for k in order:
        scatter_copy(k).start()
    for k in order:
        gather_copy(k).start()

    out_ref[...] = (pre * sig).astype(BF16)
    stores = [
        pltpu.make_async_copy(out_ref, out_hbm, out_sem.at[0]),
        pltpu.make_async_copy(fg_ref, fg_hbm, out_sem.at[1]),
    ]
    stores[0].start()
    local_sum[...] = dot(dpre, ws_ref[...], 1, 1) + dot(dense_t[0], gsend[...])

    total = wsum[mine, :].astype(F32)
    for k in order:
        scatter_copy(k).wait_recv()
        total = total + dslots[k].astype(F32)
    zslots[layer] = total.astype(BF16)
    for k in range(depth - 1, 0, -1):
        layer_copy(k).start()
    for k in range(1, depth):
        layer_copy(k).wait_recv()
    total = zslots[0].astype(F32)
    for k in range(1, depth):
        total = total + zslots[k].astype(F32)
    wfull[core, mine, :] = (total * scale).astype(BF16)
    for k in order:
        spread_copy(k).start()
    finals = []

    def forward_piece(k):
        piece = wfull.at[core, pl.ds(pl.multiple_of(peers[k] * rows, rows), rows)]
        finals.append(sibling_copy(k, piece, piece))
        finals[-1].start()

    forward_piece(0)
    grad = local_sum[...]
    for k in order[::-1]:
        gather_copy(k).wait_recv()
        grad = grad + dot(dense_t[k], grecv[k])
    fg_ref[...] = grad.astype(BF16)
    stores[1].start()

    for k in order[::-1]:
        spread_copy(k).wait_recv()
        forward_piece(k)
    halves = [
        pltpu.make_async_copy(wg_ref.at[half], wg_hbm.at[half], out_sem.at[2 + i])
        for i, half in enumerate((core, 1 - core))
    ]
    wg_ref[core] = wfull[core].astype(F32)
    halves[0].start()
    for final in finals:
        final.wait_recv()
    wg_ref[1 - core] = wfull[1 - core].astype(F32)
    halves[1].start()
    halving.wait_send()
    for final in finals:
        final.wait_send()
    for k in order:
        forward_copy(k).wait_send()
        gather_copy(k).wait_send()
        scatter_copy(k).wait_send()
        spread_copy(k).wait_send()
    for k in range(1, depth):
        layer_copy(k).wait_send()
    for store in stores + halves:
        store.wait()


def finish(out_ref, fg_ref, wg_ref, out_hbm, fg_hbm, wg_hbm, out_v, fg_v, wg_v, in_sem, out_sem):
    trips = [
        (wg_ref.at[0], wg_v.at[0], wg_hbm.at[0]),
        (wg_ref.at[1], wg_v.at[1], wg_hbm.at[1]),
        (out_ref, out_v, out_hbm),
        (fg_ref, fg_v, fg_hbm),
    ]
    loads = [pltpu.make_async_copy(a, b, in_sem.at[i]) for i, (a, b, _) in enumerate(trips)]
    stores = [pltpu.make_async_copy(b, c, out_sem.at[i]) for i, (_, b, c) in enumerate(trips)]
    for load in loads:
        load.start()
    for load, store in zip(loads, stores):
        load.wait()
        store.start()
    for store in stores:
        store.wait()


def body(features, adjacency, src_tile, dst_peer, dst_tile, w_self, w_neigh, out_grad):
    nodes, width = features.shape
    parts, groups = lax.axis_size("dom"), lax.axis_size("grp")
    depth = groups // CORES
    scale = 1.0 / math.sqrt(nodes * parts * groups)
    rows = width // parts
    hbm = pl.BlockSpec(memory_space=pltpu.HBM)
    square = (nodes, width)
    dma = pltpu.SemaphoreType.DMA
    output, feat_grad, grads = pl.pallas_call(
        functools.partial(kernel, parts, depth, scale),
        out_shape=(
            jax.ShapeDtypeStruct(square, BF16),
            jax.ShapeDtypeStruct(square, BF16),
            jax.ShapeDtypeStruct((2, width, width), F32),
        ),
        in_specs=[hbm] * 8,
        out_specs=(hbm, hbm, hbm),
        scratch_shapes=[
            pltpu.SMEM(src_tile.shape, jnp.int32),
            pltpu.SMEM(src_tile.shape, jnp.int32),
            pltpu.SMEM(src_tile.shape, jnp.int32),
            pltpu.VMEM(square, BF16),
            pltpu.VMEM(adjacency.shape, BF16),
            pltpu.VMEM(w_self.shape, BF16),
            pltpu.VMEM(w_neigh.shape, BF16),
            pltpu.VMEM(square, BF16),
            pltpu.VMEM((parts, nodes, nodes), BF16),
            pltpu.VMEM((parts, nodes, nodes), BF16),
            pltpu.VMEM((parts,) + square, BF16),
            pltpu.VMEM((parts,) + square, BF16),
            pltpu.VMEM(square, BF16),
            pltpu.VMEM((parts,) + square, BF16),
            pltpu.VMEM((2, width, nodes), BF16),
            pltpu.VMEM((width, width), BF16),
            pltpu.VMEM((width, width), BF16),
            pltpu.VMEM((width, width), BF16),
            pltpu.VMEM((parts, rows, width), BF16),
            pltpu.VMEM((depth, rows, width), BF16),
            pltpu.VMEM((2, width, width), BF16),
            pltpu.VMEM(square, BF16),
            pltpu.VMEM(square, BF16),
            pltpu.VMEM((2, width, width), F32),
            pltpu.VMEM(square, F32),
            dma((8,)), dma((4,)), dma((parts,)), dma((parts,)), dma((parts,)), dma((parts,)),
            dma((parts + 1,)), dma((parts + 1,)), dma((parts,)), dma((parts,)),
            dma((depth,)), dma((depth,)), dma((parts,)), dma((parts,)),
        ],
        compiler_params=pltpu.CompilerParams(
            collective_id=0, has_side_effects=True, vmem_limit_bytes=VMEM_BYTES
        ),
        name="sage_layer",
    )(src_tile, dst_peer[:, 0], dst_tile, features, adjacency, w_self, w_neigh, out_grad)
    return pl.pallas_call(
        finish,
        out_shape=(
            jax.ShapeDtypeStruct(square, BF16),
            jax.ShapeDtypeStruct(square, BF16),
            jax.ShapeDtypeStruct((2, width, width), F32),
        ),
        in_specs=[hbm] * 3,
        out_specs=(hbm, hbm, hbm),
        scratch_shapes=[
            pltpu.VMEM(square, BF16),
            pltpu.VMEM(square, BF16),
            pltpu.VMEM((2, width, width), F32),
            dma((4,)), dma((4,)),
        ],
        compiler_params=pltpu.CompilerParams(vmem_limit_bytes=VMEM_BYTES),
        name="write_results",
    )(output, feat_grad, grads)


def solution(mesh):
    shard = ("dom", "grp")
    in_specs = (
        P(shard, None),
        P(shard, None, None),
        P(shard),
        P(shard, None),
        P(shard),
        P(),
        P(),
        P(shard, None),
    )
    out_specs = (P(shard, None), P(shard, None), P())
    return jax.shard_map(body, mesh=mesh, in_specs=in_specs, out_specs=out_specs, check_vma=False)
```

```python
import functools
import math

import jax
import jax.numpy as jnp
from jax import lax
from jax.experimental import pallas as pl
from jax.experimental.pallas import tpu as pltpu
from jax.sharding import PartitionSpec as P

MESH = pl.DeviceIdType.MESH
BF16 = jnp.bfloat16
F32 = jnp.float32
STRIP = 32
CORES = 2
VMEM_BYTES = 63 * 1024 * 1024


def dot(a, b, ca=1, cb=0):
    return lax.dot_general(a, b, (((ca,), (cb,)), ((), ())), preferred_element_type=F32)


def flip(index, k, size):
    total, bit = 0, 1
    while bit < size:
        digit = lax.rem(index // bit, 2)
        total = total + bit * ((1 - digit) if (k // bit) % 2 else digit)
        bit *= 2
    return total


def kernel(
    parts, depth, scale,
    src_hbm, peer_hbm, tile_hbm, x_hbm, adj_hbm, ws_hbm, wn_hbm, og_hbm,
    out_hbm, fg_hbm, wg_hbm,
    src_ref, peer_ref, tile_ref, x_ref, adj_ref, ws_ref, wn_ref, og_ref,
    dense, dense_t, fsend, frecv, gsend, grecv, both_t, wsend, wsib, wsum, dslots, zslots, wfull, out_ref, fg_ref, wg_ref, local_sum,
    in_sem, out_sem, fs_sem, fr_sem, gs_sem, gr_sem, sib_s, sib_r, rs_s, rs_r, z_s, z_r, ag_s, ag_r,
):
    dom = lax.axis_index("dom")
    grp = lax.axis_index("grp")
    count, tile = adj_ref.shape[0], adj_ref.shape[1]
    nodes, width = x_ref.shape
    nt = nodes // tile
    core = lax.rem(grp, CORES)
    layer = grp // CORES
    rows = width // parts
    sibling = (dom, layer * CORES + (1 - core))

    loads = [
        pltpu.make_async_copy(hbm, local, in_sem.at[i])
        for i, (hbm, local) in enumerate([
            (peer_hbm, peer_ref), (tile_hbm, tile_ref), (src_hbm, src_ref), (adj_hbm, adj_ref),
            (x_hbm, x_ref), (ws_hbm, ws_ref), (wn_hbm, wn_ref), (og_hbm, og_ref),
        ])
    ]
    for load in loads:
        load.start()

    peers = [flip(dom, k, parts) for k in range(parts)]

    layers = [(dom, flip(layer, k, depth) * CORES + core) for k in range(depth)]

    barrier = pltpu.get_barrier_semaphore()
    partners = [(peers[k], grp) for k in range(1, parts)] + layers[1:] + [sibling]
    for partner in partners:
        pl.semaphore_signal(barrier, inc=1, device_id=partner, device_id_type=MESH)

    for load in loads[:5]:
        load.wait()
    codes = [(peer_ref[t] * nt + tile_ref[t]) * nt + src_ref[t] for t in range(count)]

    def build(k):
        base = peers[k] * (nt * nt)
        marks = [
            [jnp.where(code - base == c, 1.0, 0.0).astype(F32) for c in range(nt * nt)]
            for code in codes
        ]

        def strip(i, carry):
            start = pl.multiple_of(i * STRIP, STRIP)
            sums = [jnp.zeros((STRIP, tile), F32) for _ in range(nt * nt)]
            for t in range(count):
                block = adj_ref[t, pl.ds(start, STRIP), :].astype(F32)
                for c in range(nt * nt):
                    sums[c] = sums[c] + marks[t][c] * block
            for c in range(nt * nt):
                rows = pl.ds((c // nt) * tile + start, STRIP)
                cols = pl.ds((c % nt) * tile, tile)
                dense[k, rows, cols] = sums[c].astype(BF16)
            return carry

        lax.fori_loop(0, tile // STRIP, strip, 0)

    def forward_copy(k):
        return pltpu.make_async_remote_copy(
            src_ref=fsend.at[k], dst_ref=frecv.at[k], send_sem=fs_sem.at[k], recv_sem=fr_sem.at[k],
            device_id=(peers[k], grp), device_id_type=MESH,
        )

    def gather_copy(k):
        return pltpu.make_async_remote_copy(
            src_ref=gsend, dst_ref=grecv.at[k], send_sem=gs_sem.at[k], recv_sem=gr_sem.at[k],
            device_id=(peers[k], grp), device_id_type=MESH,
        )

    half = nodes // 2
    lower, upper = pl.ds(0, half), pl.ds(half, half)

    def hop(src, dst, i, send, recv, k):
        return pltpu.make_async_remote_copy(
            src_ref=src, dst_ref=dst, send_sem=send.at[i], recv_sem=recv.at[i],
            device_id=(peers[k], grp), device_id_type=MESH,
        )

    relayed = parts == 4
    if relayed:
        forward_hops = [
            hop(fsend.at[3, lower], frecv.at[3, lower], 0, fs_sem, fr_sem, 1),
            hop(fsend.at[3, upper], frecv.at[3, upper], 1, fs_sem, fr_sem, 2),
            hop(fsend.at[1, lower], frecv.at[1, lower], 2, fs_sem, fr_sem, 1),
            hop(fsend.at[2, upper], frecv.at[2, upper], 3, fs_sem, fr_sem, 2),
            hop(fsend.at[1, upper], frecv.at[1, upper], 4, fs_sem, fr_sem, 1),
            hop(fsend.at[2, lower], frecv.at[2, lower], 5, fs_sem, fr_sem, 2),
        ]
        gather_hops = [
            hop(gsend.at[lower], grecv.at[1, lower], 0, gs_sem, gr_sem, 1),
            hop(gsend.at[upper], grecv.at[2, upper], 1, gs_sem, gr_sem, 2),
            hop(gsend.at[upper], grecv.at[1, upper], 2, gs_sem, gr_sem, 1),
            hop(gsend.at[lower], grecv.at[2, lower], 3, gs_sem, gr_sem, 2),
            hop(grecv.at[2, upper], grecv.at[3, upper], 4, gs_sem, gr_sem, 1),
            hop(grecv.at[1, lower], grecv.at[3, lower], 5, gs_sem, gr_sem, 2),
        ]
    else:
        forward_hops = [forward_copy(k) for k in range(1, parts)]
        gather_hops = [gather_copy(k) for k in range(1, parts)]

    x = x_ref[...]
    order = list(range(parts - 1, 0, -1))
    if relayed:
        build(3)
        fsend[3] = dot(dense[3], x).astype(BF16)
        pl.semaphore_wait(barrier, len(partners))
        forward_hops[0].start()
        forward_hops[1].start()
        build(1)
        to_one = dot(dense[1], x)
        fsend[1, :half] = to_one[:half].astype(BF16)
        forward_hops[2].start()
        build(2)
        to_two = dot(dense[2], x)
        fsend[2, half:] = to_two[half:].astype(BF16)
        forward_hops[3].start()
        forward_hops[1].wait_recv()
        fsend[1, half:] = (to_one[half:] + frecv[3, half:].astype(F32)).astype(BF16)
        forward_hops[4].start()
        forward_hops[0].wait_recv()
        fsend[2, :half] = (to_two[:half] + frecv[3, :half].astype(F32)).astype(BF16)
        forward_hops[5].start()
    else:
        for k in order:
            build(k)
            fsend[k] = dot(dense[k], x).astype(BF16)
            if k == order[0]:
                pl.semaphore_wait(barrier, len(partners))
            forward_hops[k - 1].start()
    build(0)
    for load in loads[5:]:
        load.wait()
    agg = dot(dense[0], x)
    pre_self = dot(x, ws_ref[...])
    both_t[0] = x.T
    for k in range(parts):
        dense_t[k] = dense[k].T
    if relayed:
        for copy in forward_hops[2:]:
            copy.wait_recv()
        agg = agg + frecv[1].astype(F32) + frecv[2].astype(F32)
    else:
        for k in order:
            forward_hops[k - 1].wait_recv()
            agg = agg + frecv[k].astype(F32)
    agg_low = agg.astype(BF16)
    both_t[1] = agg_low.T
    pre = pre_self + dot(agg_low, wn_ref[...])
    sig = jax.nn.sigmoid(pre)
    dpre = (og_ref[...].astype(F32) * sig * (1.0 + pre * (1.0 - sig))).astype(BF16)

    def sibling_copy(i, src, dst):
        return pltpu.make_async_remote_copy(
            src_ref=src, dst_ref=dst, send_sem=sib_s.at[i], recv_sem=sib_r.at[i],
            device_id=sibling, device_id_type=MESH,
        )

    halving = sibling_copy(parts, wsend, wsib)
    wsend[...] = dot(both_t[1 - core], dpre).astype(BF16)
    halving.start()
    gsend[...] = dot(dpre, wn_ref[...], 1, 1).astype(BF16)
    own = dot(both_t[core], dpre)

    def scatter_copy(k):
        start = pl.multiple_of(peers[k] * rows, rows)
        return pltpu.make_async_remote_copy(
            src_ref=wsum.at[pl.ds(start, rows)], dst_ref=dslots.at[k], send_sem=rs_s.at[k],
            recv_sem=rs_r.at[k], device_id=(peers[k], grp), device_id_type=MESH,
        )

    def layer_copy(k):
        return pltpu.make_async_remote_copy(
            src_ref=zslots.at[layer], dst_ref=zslots.at[layer], send_sem=z_s.at[k],
            recv_sem=z_r.at[k], device_id=layers[k], device_id_type=MESH,
        )

    mine = pl.ds(pl.multiple_of(dom * rows, rows), rows)

    def spread_copy(k):
        return pltpu.make_async_remote_copy(
            src_ref=wfull.at[core, mine], dst_ref=wfull.at[core, mine], send_sem=ag_s.at[k],
            recv_sem=ag_r.at[k], device_id=(peers[k], grp), device_id_type=MESH,
        )

    halving.wait_recv()
    wsum[...] = (own + wsib[...].astype(F32)).astype(BF16)
    for k in order:
        scatter_copy(k).start()
    for copy in gather_hops[:4] if relayed else gather_hops:
        copy.start()

    out_ref[...] = (pre * sig).astype(BF16)
    stores = [
        pltpu.make_async_copy(out_ref, out_hbm, out_sem.at[0]),
        pltpu.make_async_copy(fg_ref, fg_hbm, out_sem.at[1]),
    ]
    stores[0].start()
    local_sum[...] = dot(dpre, ws_ref[...], 1, 1) + dot(dense_t[0], gsend[...])

    total = wsum[mine, :].astype(F32)
    for k in order:
        scatter_copy(k).wait_recv()
        total = total + dslots[k].astype(F32)
    zslots[layer] = total.astype(BF16)
    for k in range(depth - 1, 0, -1):
        layer_copy(k).start()
    if relayed:
        gather_hops[1].wait_recv()
        gather_hops[4].start()
        gather_hops[0].wait_recv()
        gather_hops[5].start()
    for k in range(1, depth):
        layer_copy(k).wait_recv()
    total = zslots[0].astype(F32)
    for k in range(1, depth):
        total = total + zslots[k].astype(F32)
    wfull[core, mine, :] = (total * scale).astype(BF16)
    for k in order:
        spread_copy(k).start()
    finals = []

    def forward_piece(k):
        piece = wfull.at[core, pl.ds(pl.multiple_of(peers[k] * rows, rows), rows)]
        finals.append(sibling_copy(k, piece, piece))
        finals[-1].start()

    forward_piece(0)
    grad = local_sum[...]
    for copy in gather_hops[2:] if relayed else gather_hops:
        copy.wait_recv()
    for k in range(1, parts):
        grad = grad + dot(dense_t[k], grecv[k])
    fg_ref[...] = grad.astype(BF16)
    stores[1].start()

    for k in order[::-1]:
        spread_copy(k).wait_recv()
        forward_piece(k)
    halves = [
        pltpu.make_async_copy(wg_ref.at[half], wg_hbm.at[half], out_sem.at[2 + i])
        for i, half in enumerate((core, 1 - core))
    ]
    wg_ref[core] = wfull[core].astype(F32)
    halves[0].start()
    for final in finals:
        final.wait_recv()
    wg_ref[1 - core] = wfull[1 - core].astype(F32)
    halves[1].start()
    halving.wait_send()
    for final in finals:
        final.wait_send()
    for k in order:
        scatter_copy(k).wait_send()
        spread_copy(k).wait_send()
    for copy in forward_hops + gather_hops:
        copy.wait_send()
    for k in range(1, depth):
        layer_copy(k).wait_send()
    for store in stores + halves:
        store.wait()


def finish(out_ref, fg_ref, wg_ref, out_hbm, fg_hbm, wg_hbm, out_v, fg_v, wg_v, in_sem, out_sem):
    trips = [
        (wg_ref.at[0], wg_v.at[0], wg_hbm.at[0]),
        (wg_ref.at[1], wg_v.at[1], wg_hbm.at[1]),
        (out_ref, out_v, out_hbm),
        (fg_ref, fg_v, fg_hbm),
    ]
    loads = [pltpu.make_async_copy(a, b, in_sem.at[i]) for i, (a, b, _) in enumerate(trips)]
    stores = [pltpu.make_async_copy(b, c, out_sem.at[i]) for i, (_, b, c) in enumerate(trips)]
    for load in loads:
        load.start()
    for load, store in zip(loads, stores):
        load.wait()
        store.start()
    for store in stores:
        store.wait()


def body(features, adjacency, src_tile, dst_peer, dst_tile, w_self, w_neigh, out_grad):
    nodes, width = features.shape
    parts, groups = lax.axis_size("dom"), lax.axis_size("grp")
    depth = groups // CORES
    scale = 1.0 / math.sqrt(nodes * parts * groups)
    rows = width // parts
    hops = max(parts, 6)
    hbm = pl.BlockSpec(memory_space=pltpu.HBM)
    square = (nodes, width)
    dma = pltpu.SemaphoreType.DMA
    output, feat_grad, grads = pl.pallas_call(
        functools.partial(kernel, parts, depth, scale),
        out_shape=(
            jax.ShapeDtypeStruct(square, BF16),
            jax.ShapeDtypeStruct(square, BF16),
            jax.ShapeDtypeStruct((2, width, width), F32),
        ),
        in_specs=[hbm] * 8,
        out_specs=(hbm, hbm, hbm),
        scratch_shapes=[
            pltpu.SMEM(src_tile.shape, jnp.int32),
            pltpu.SMEM(src_tile.shape, jnp.int32),
            pltpu.SMEM(src_tile.shape, jnp.int32),
            pltpu.VMEM(square, BF16),
            pltpu.VMEM(adjacency.shape, BF16),
            pltpu.VMEM(w_self.shape, BF16),
            pltpu.VMEM(w_neigh.shape, BF16),
            pltpu.VMEM(square, BF16),
            pltpu.VMEM((parts, nodes, nodes), BF16),
            pltpu.VMEM((parts, nodes, nodes), BF16),
            pltpu.VMEM((parts,) + square, BF16),
            pltpu.VMEM((parts,) + square, BF16),
            pltpu.VMEM(square, BF16),
            pltpu.VMEM((parts,) + square, BF16),
            pltpu.VMEM((2, width, nodes), BF16),
            pltpu.VMEM((width, width), BF16),
            pltpu.VMEM((width, width), BF16),
            pltpu.VMEM((width, width), BF16),
            pltpu.VMEM((parts, rows, width), BF16),
            pltpu.VMEM((depth, rows, width), BF16),
            pltpu.VMEM((2, width, width), BF16),
            pltpu.VMEM(square, BF16),
            pltpu.VMEM(square, BF16),
            pltpu.VMEM((2, width, width), F32),
            pltpu.VMEM(square, F32),
            dma((8,)), dma((4,)), dma((hops,)), dma((hops,)), dma((hops,)), dma((hops,)),
            dma((parts + 1,)), dma((parts + 1,)), dma((parts,)), dma((parts,)),
            dma((depth,)), dma((depth,)), dma((parts,)), dma((parts,)),
        ],
        compiler_params=pltpu.CompilerParams(
            collective_id=0, has_side_effects=True, vmem_limit_bytes=VMEM_BYTES
        ),
        name="sage_layer",
    )(src_tile, dst_peer[:, 0], dst_tile, features, adjacency, w_self, w_neigh, out_grad)
    return pl.pallas_call(
        finish,
        out_shape=(
            jax.ShapeDtypeStruct(square, BF16),
            jax.ShapeDtypeStruct(square, BF16),
            jax.ShapeDtypeStruct((2, width, width), F32),
        ),
        in_specs=[hbm] * 3,
        out_specs=(hbm, hbm, hbm),
        scratch_shapes=[
            pltpu.VMEM(square, BF16),
            pltpu.VMEM(square, BF16),
            pltpu.VMEM((2, width, width), F32),
            dma((4,)), dma((4,)),
        ],
        compiler_params=pltpu.CompilerParams(vmem_limit_bytes=VMEM_BYTES),
        name="write_results",
    )(output, feat_grad, grads)


def solution(mesh):
    shard = ("dom", "grp")
    in_specs = (
        P(shard, None),
        P(shard, None, None),
        P(shard),
        P(shard, None),
        P(shard),
        P(),
        P(),
        P(shard, None),
    )
    out_specs = (P(shard, None), P(shard, None), P())
    return jax.shard_map(body, mesh=mesh, in_specs=in_specs, out_specs=out_specs, check_vma=False)
```

```python
import functools
import math

import jax
import jax.numpy as jnp
from jax import lax
from jax.experimental import pallas as pl
from jax.experimental.pallas import tpu as pltpu
from jax.sharding import PartitionSpec as P

MESH = pl.DeviceIdType.MESH
BF16 = jnp.bfloat16
F32 = jnp.float32
CORES = 2
VMEM_BYTES = 63 * 1024 * 1024


def dot(a, b, ca=1, cb=0):
    return lax.dot_general(a, b, (((ca,), (cb,)), ((), ())), preferred_element_type=F32)


def flip(index, k, size):
    total, bit = 0, 1
    while bit < size:
        digit = lax.rem(index // bit, 2)
        total = total + bit * ((1 - digit) if (k // bit) % 2 else digit)
        bit *= 2
    return total


def kernel(
    parts, depth, scale,
    src_hbm, peer_hbm, tile_hbm, x_hbm, adj_hbm, ws_hbm, wn_hbm, og_hbm,
    out_hbm, fg_hbm, wg_hbm,
    src_ref, peer_ref, tile_ref, x_ref, adj_ref, ws_ref, wn_ref, og_ref,
    runs, dense, dense_t, fsend, frecv, gsend, grecv, both_t, wsend, wsib, wsum, dslots, zslots, wfull, out_ref, fg_ref, wg_ref, local_sum,
    in_sem, out_sem, fs_sem, fr_sem, gs_sem, gr_sem, sib_s, sib_r, rs_s, rs_r, z_s, z_r, ag_s, ag_r,
):
    dom = lax.axis_index("dom")
    grp = lax.axis_index("grp")
    count, tile = adj_ref.shape[0], adj_ref.shape[1]
    nodes, width = x_ref.shape
    nt = nodes // tile
    core = lax.rem(grp, CORES)
    layer = grp // CORES
    rows = width // parts
    sibling = (dom, layer * CORES + (1 - core))

    loads = [
        pltpu.make_async_copy(hbm, local, in_sem.at[i])
        for i, (hbm, local) in enumerate([
            (peer_hbm, peer_ref), (tile_hbm, tile_ref), (src_hbm, src_ref), (adj_hbm, adj_ref),
            (x_hbm, x_ref), (ws_hbm, ws_ref), (wn_hbm, wn_ref), (og_hbm, og_ref),
        ])
    ]
    for load in loads:
        load.start()

    peers = [flip(dom, k, parts) for k in range(parts)]

    layers = [(dom, flip(layer, k, depth) * CORES + core) for k in range(depth)]

    barrier = pltpu.get_barrier_semaphore()
    partners = [(peers[k], grp) for k in range(1, parts)] + layers[1:] + [sibling]
    for partner in partners:
        pl.semaphore_signal(barrier, inc=1, device_id=partner, device_id_type=MESH)

    for load in loads[:3]:
        load.wait()
    codes = [(peer_ref[t] * nt + tile_ref[t]) * nt + src_ref[t] for t in range(count)]
    earlier = []
    for t in range(count):
        slot = jnp.int32(0)
        for u in range(t):
            slot = jnp.where(codes[u] == codes[t], u + 1, slot)
        earlier.append(slot)
    latest = {}
    for k in range(parts):
        for c in range(nt * nt):
            slot = jnp.int32(0)
            for t in range(count):
                slot = jnp.where(codes[t] == peers[k] * (nt * nt) + c, t + 1, slot)
            latest[k, c] = slot
    runs[0] = jnp.zeros((tile, tile), F32)
    for load in loads[3:5]:
        load.wait()
    for t in range(count):
        runs[t + 1] = runs[earlier[t]] + adj_ref[t].astype(F32)

    def build(k):
        for c in range(nt * nt):
            rows_here = pl.ds((c // nt) * tile, tile)
            cols_here = pl.ds((c % nt) * tile, tile)
            dense[k, rows_here, cols_here] = runs[latest[k, c]].astype(BF16)

    def forward_copy(k):
        return pltpu.make_async_remote_copy(
            src_ref=fsend.at[k], dst_ref=frecv.at[k], send_sem=fs_sem.at[k], recv_sem=fr_sem.at[k],
            device_id=(peers[k], grp), device_id_type=MESH,
        )

    def gather_copy(k):
        return pltpu.make_async_remote_copy(
            src_ref=gsend, dst_ref=grecv.at[k], send_sem=gs_sem.at[k], recv_sem=gr_sem.at[k],
            device_id=(peers[k], grp), device_id_type=MESH,
        )

    half = nodes // 2
    lower, upper = pl.ds(0, half), pl.ds(half, half)

    def hop(src, dst, i, send, recv, k):
        return pltpu.make_async_remote_copy(
            src_ref=src, dst_ref=dst, send_sem=send.at[i], recv_sem=recv.at[i],
            device_id=(peers[k], grp), device_id_type=MESH,
        )

    relayed = parts == 4
    if relayed:
        forward_hops = [
            hop(fsend.at[3, lower], frecv.at[3, lower], 0, fs_sem, fr_sem, 1),
            hop(fsend.at[3, upper], frecv.at[3, upper], 1, fs_sem, fr_sem, 2),
            hop(fsend.at[1, lower], frecv.at[1, lower], 2, fs_sem, fr_sem, 1),
            hop(fsend.at[2, upper], frecv.at[2, upper], 3, fs_sem, fr_sem, 2),
            hop(fsend.at[1, upper], frecv.at[1, upper], 4, fs_sem, fr_sem, 1),
            hop(fsend.at[2, lower], frecv.at[2, lower], 5, fs_sem, fr_sem, 2),
        ]
        gather_hops = [
            hop(gsend.at[lower], grecv.at[1, lower], 0, gs_sem, gr_sem, 1),
            hop(gsend.at[upper], grecv.at[2, upper], 1, gs_sem, gr_sem, 2),
            hop(gsend.at[upper], grecv.at[1, upper], 2, gs_sem, gr_sem, 1),
            hop(gsend.at[lower], grecv.at[2, lower], 3, gs_sem, gr_sem, 2),
            hop(grecv.at[2, upper], grecv.at[3, upper], 4, gs_sem, gr_sem, 1),
            hop(grecv.at[1, lower], grecv.at[3, lower], 5, gs_sem, gr_sem, 2),
        ]
    else:
        forward_hops = [forward_copy(k) for k in range(1, parts)]
        gather_hops = [gather_copy(k) for k in range(1, parts)]

    x = x_ref[...]
    order = list(range(parts - 1, 0, -1))
    if relayed:
        build(3)
        fsend[3] = dot(dense[3], x).astype(BF16)
        pl.semaphore_wait(barrier, len(partners))
        forward_hops[0].start()
        forward_hops[1].start()
        build(1)
        to_one = dot(dense[1], x)
        fsend[1, :half] = to_one[:half].astype(BF16)
        forward_hops[2].start()
        build(2)
        to_two = dot(dense[2], x)
        fsend[2, half:] = to_two[half:].astype(BF16)
        forward_hops[3].start()
        forward_hops[1].wait_recv()
        fsend[1, half:] = (to_one[half:] + frecv[3, half:].astype(F32)).astype(BF16)
        forward_hops[4].start()
        forward_hops[0].wait_recv()
        fsend[2, :half] = (to_two[:half] + frecv[3, :half].astype(F32)).astype(BF16)
        forward_hops[5].start()
    else:
        for k in order:
            build(k)
            fsend[k] = dot(dense[k], x).astype(BF16)
            if k == order[0]:
                pl.semaphore_wait(barrier, len(partners))
            forward_hops[k - 1].start()
    build(0)
    for load in loads[5:]:
        load.wait()
    agg = dot(dense[0], x)
    pre_self = dot(x, ws_ref[...])
    both_t[0] = x.T
    for k in range(parts):
        dense_t[k] = dense[k].T
    if relayed:
        for copy in forward_hops[2:]:
            copy.wait_recv()
        agg = agg + frecv[1].astype(F32) + frecv[2].astype(F32)
    else:
        for k in order:
            forward_hops[k - 1].wait_recv()
            agg = agg + frecv[k].astype(F32)
    agg_low = agg.astype(BF16)
    both_t[1] = agg_low.T
    pre = pre_self + dot(agg_low, wn_ref[...])
    sig = jax.nn.sigmoid(pre)
    dpre = (og_ref[...].astype(F32) * sig * (1.0 + pre * (1.0 - sig))).astype(BF16)

    def sibling_copy(i, src, dst):
        return pltpu.make_async_remote_copy(
            src_ref=src, dst_ref=dst, send_sem=sib_s.at[i], recv_sem=sib_r.at[i],
            device_id=sibling, device_id_type=MESH,
        )

    halving = sibling_copy(parts, wsend, wsib)
    wsend[...] = dot(both_t[1 - core], dpre).astype(BF16)
    halving.start()
    gsend[...] = dot(dpre, wn_ref[...], 1, 1).astype(BF16)
    own = dot(both_t[core], dpre)

    def scatter_copy(k):
        start = pl.multiple_of(peers[k] * rows, rows)
        return pltpu.make_async_remote_copy(
            src_ref=wsum.at[pl.ds(start, rows)], dst_ref=dslots.at[k], send_sem=rs_s.at[k],
            recv_sem=rs_r.at[k], device_id=(peers[k], grp), device_id_type=MESH,
        )

    def layer_copy(k):
        return pltpu.make_async_remote_copy(
            src_ref=zslots.at[layer], dst_ref=zslots.at[layer], send_sem=z_s.at[k],
            recv_sem=z_r.at[k], device_id=layers[k], device_id_type=MESH,
        )

    mine = pl.ds(pl.multiple_of(dom * rows, rows), rows)

    def spread_copy(k):
        return pltpu.make_async_remote_copy(
            src_ref=wfull.at[core, mine], dst_ref=wfull.at[core, mine], send_sem=ag_s.at[k],
            recv_sem=ag_r.at[k], device_id=(peers[k], grp), device_id_type=MESH,
        )

    halving.wait_recv()
    wsum[...] = (own + wsib[...].astype(F32)).astype(BF16)
    for k in order:
        scatter_copy(k).start()
    for copy in gather_hops[:4] if relayed else gather_hops:
        copy.start()

    out_ref[...] = (pre * sig).astype(BF16)
    stores = [
        pltpu.make_async_copy(out_ref, out_hbm, out_sem.at[0]),
        pltpu.make_async_copy(fg_ref, fg_hbm, out_sem.at[1]),
    ]
    stores[0].start()
    local_sum[...] = dot(dpre, ws_ref[...], 1, 1) + dot(dense_t[0], gsend[...])

    total = wsum[mine, :].astype(F32)
    for k in order:
        scatter_copy(k).wait_recv()
        total = total + dslots[k].astype(F32)
    zslots[layer] = total.astype(BF16)
    for k in range(depth - 1, 0, -1):
        layer_copy(k).start()
    if relayed:
        gather_hops[1].wait_recv()
        gather_hops[4].start()
        gather_hops[0].wait_recv()
        gather_hops[5].start()
    for k in range(1, depth):
        layer_copy(k).wait_recv()
    total = zslots[0].astype(F32)
    for k in range(1, depth):
        total = total + zslots[k].astype(F32)
    wfull[core, mine, :] = (total * scale).astype(BF16)
    for k in order:
        spread_copy(k).start()
    finals = []

    def forward_piece(k):
        piece = wfull.at[core, pl.ds(pl.multiple_of(peers[k] * rows, rows), rows)]
        finals.append(sibling_copy(k, piece, piece))
        finals[-1].start()

    forward_piece(0)
    grad = local_sum[...]
    for copy in gather_hops[2:] if relayed else gather_hops:
        copy.wait_recv()
    for k in range(1, parts):
        grad = grad + dot(dense_t[k], grecv[k])
    fg_ref[...] = grad.astype(BF16)
    stores[1].start()

    for k in order[::-1]:
        spread_copy(k).wait_recv()
        forward_piece(k)
    halves = [
        pltpu.make_async_copy(wg_ref.at[half], wg_hbm.at[half], out_sem.at[2 + i])
        for i, half in enumerate((core, 1 - core))
    ]
    wg_ref[core] = wfull[core].astype(F32)
    halves[0].start()
    for final in finals:
        final.wait_recv()
    wg_ref[1 - core] = wfull[1 - core].astype(F32)
    halves[1].start()
    halving.wait_send()
    for final in finals:
        final.wait_send()
    for k in order:
        scatter_copy(k).wait_send()
        spread_copy(k).wait_send()
    for copy in forward_hops + gather_hops:
        copy.wait_send()
    for k in range(1, depth):
        layer_copy(k).wait_send()
    for store in stores + halves:
        store.wait()


def finish(out_ref, fg_ref, wg_ref, out_hbm, fg_hbm, wg_hbm, out_v, fg_v, wg_v, in_sem, out_sem):
    trips = [
        (wg_ref.at[0], wg_v.at[0], wg_hbm.at[0]),
        (wg_ref.at[1], wg_v.at[1], wg_hbm.at[1]),
        (out_ref, out_v, out_hbm),
        (fg_ref, fg_v, fg_hbm),
    ]
    loads = [pltpu.make_async_copy(a, b, in_sem.at[i]) for i, (a, b, _) in enumerate(trips)]
    stores = [pltpu.make_async_copy(b, c, out_sem.at[i]) for i, (_, b, c) in enumerate(trips)]
    for load in loads:
        load.start()
    for load, store in zip(loads, stores):
        load.wait()
        store.start()
    for store in stores:
        store.wait()


def body(features, adjacency, src_tile, dst_peer, dst_tile, w_self, w_neigh, out_grad):
    nodes, width = features.shape
    count, tile = adjacency.shape[:2]
    parts, groups = lax.axis_size("dom"), lax.axis_size("grp")
    depth = groups // CORES
    scale = 1.0 / math.sqrt(nodes * parts * groups)
    rows = width // parts
    hops = max(parts, 6)
    hbm = pl.BlockSpec(memory_space=pltpu.HBM)
    square = (nodes, width)
    dma = pltpu.SemaphoreType.DMA
    output, feat_grad, grads = pl.pallas_call(
        functools.partial(kernel, parts, depth, scale),
        out_shape=(
            jax.ShapeDtypeStruct(square, BF16),
            jax.ShapeDtypeStruct(square, BF16),
            jax.ShapeDtypeStruct((2, width, width), F32),
        ),
        in_specs=[hbm] * 8,
        out_specs=(hbm, hbm, hbm),
        scratch_shapes=[
            pltpu.SMEM(src_tile.shape, jnp.int32),
            pltpu.SMEM(src_tile.shape, jnp.int32),
            pltpu.SMEM(src_tile.shape, jnp.int32),
            pltpu.VMEM(square, BF16),
            pltpu.VMEM(adjacency.shape, BF16),
            pltpu.VMEM(w_self.shape, BF16),
            pltpu.VMEM(w_neigh.shape, BF16),
            pltpu.VMEM(square, BF16),
            pltpu.VMEM((count + 1, tile, tile), F32),
            pltpu.VMEM((parts, nodes, nodes), BF16),
            pltpu.VMEM((parts, nodes, nodes), BF16),
            pltpu.VMEM((parts,) + square, BF16),
            pltpu.VMEM((parts,) + square, BF16),
            pltpu.VMEM(square, BF16),
            pltpu.VMEM((parts,) + square, BF16),
            pltpu.VMEM((2, width, nodes), BF16),
            pltpu.VMEM((width, width), BF16),
            pltpu.VMEM((width, width), BF16),
            pltpu.VMEM((width, width), BF16),
            pltpu.VMEM((parts, rows, width), BF16),
            pltpu.VMEM((depth, rows, width), BF16),
            pltpu.VMEM((2, width, width), BF16),
            pltpu.VMEM(square, BF16),
            pltpu.VMEM(square, BF16),
            pltpu.VMEM((2, width, width), F32),
            pltpu.VMEM(square, F32),
            dma((8,)), dma((4,)), dma((hops,)), dma((hops,)), dma((hops,)), dma((hops,)),
            dma((parts + 1,)), dma((parts + 1,)), dma((parts,)), dma((parts,)),
            dma((depth,)), dma((depth,)), dma((parts,)), dma((parts,)),
        ],
        compiler_params=pltpu.CompilerParams(
            collective_id=0, has_side_effects=True, vmem_limit_bytes=VMEM_BYTES
        ),
        name="sage_layer",
    )(src_tile, dst_peer[:, 0], dst_tile, features, adjacency, w_self, w_neigh, out_grad)
    return pl.pallas_call(
        finish,
        out_shape=(
            jax.ShapeDtypeStruct(square, BF16),
            jax.ShapeDtypeStruct(square, BF16),
            jax.ShapeDtypeStruct((2, width, width), F32),
        ),
        in_specs=[hbm] * 3,
        out_specs=(hbm, hbm, hbm),
        scratch_shapes=[
            pltpu.VMEM(square, BF16),
            pltpu.VMEM(square, BF16),
            pltpu.VMEM((2, width, width), F32),
            dma((4,)), dma((4,)),
        ],
        compiler_params=pltpu.CompilerParams(vmem_limit_bytes=VMEM_BYTES),
        name="write_results",
    )(output, feat_grad, grads)


def solution(mesh):
    shard = ("dom", "grp")
    in_specs = (
        P(shard, None),
        P(shard, None, None),
        P(shard),
        P(shard, None),
        P(shard),
        P(),
        P(),
        P(shard, None),
    )
    out_specs = (P(shard, None), P(shard, None), P())
    return jax.shard_map(body, mesh=mesh, in_specs=in_specs, out_specs=out_specs, check_vma=False)
```

```python
import functools
import math

import jax
import jax.numpy as jnp
from jax import lax
from jax.experimental import pallas as pl
from jax.experimental.pallas import tpu as pltpu
from jax.sharding import PartitionSpec as P

MESH = pl.DeviceIdType.MESH
BF16 = jnp.bfloat16
F32 = jnp.float32
CORES = 2
VMEM_BYTES = 63 * 1024 * 1024


def dot(a, b, ca=1, cb=0):
    return lax.dot_general(a, b, (((ca,), (cb,)), ((), ())), preferred_element_type=F32)


def flip(index, k, size):
    total, bit = 0, 1
    while bit < size:
        digit = lax.rem(index // bit, 2)
        total = total + bit * ((1 - digit) if (k // bit) % 2 else digit)
        bit *= 2
    return total


def kernel(
    parts, depth, scale,
    src_hbm, peer_hbm, tile_hbm, x_hbm, adj_hbm, ws_hbm, wn_hbm, og_hbm,
    out_hbm, fg_hbm, wg_hbm,
    src_ref, peer_ref, tile_ref, x_ref, adj_ref, ws_ref, wn_ref, og_ref,
    runs, dense, dense_t, fsend, frecv, gsend, grecv, both_t, wsend, wsib, wsum, dslots, zslots, wfull, out_ref, fg_ref, wg_ref, local_sum,
    in_sem, out_sem, fs_sem, fr_sem, gs_sem, gr_sem, sib_s, sib_r, rs_s, rs_r, z_s, z_r, ag_s, ag_r,
):
    dom = lax.axis_index("dom")
    grp = lax.axis_index("grp")
    count, tile = adj_ref.shape[0], adj_ref.shape[1]
    nodes, width = x_ref.shape
    nt = nodes // tile
    core = lax.rem(grp, CORES)
    layer = grp // CORES
    rows = width // parts
    sibling = (dom, layer * CORES + (1 - core))

    loads = [
        pltpu.make_async_copy(hbm, local, in_sem.at[i])
        for i, (hbm, local) in enumerate([
            (peer_hbm, peer_ref), (tile_hbm, tile_ref), (src_hbm, src_ref), (adj_hbm, adj_ref),
            (x_hbm, x_ref), (ws_hbm, ws_ref), (wn_hbm, wn_ref), (og_hbm, og_ref),
        ])
    ]
    for load in loads:
        load.start()

    peers = [flip(dom, k, parts) for k in range(parts)]

    layers = [(dom, flip(layer, k, depth) * CORES + core) for k in range(depth)]

    barrier = pltpu.get_barrier_semaphore()
    partners = [(peers[k], grp) for k in range(1, parts)] + layers[1:] + [sibling]
    for partner in partners:
        pl.semaphore_signal(barrier, inc=1, device_id=partner, device_id_type=MESH)

    for load in loads[:3]:
        load.wait()
    codes = [(peer_ref[t] * nt + tile_ref[t]) * nt + src_ref[t] for t in range(count)]
    earlier = []
    for t in range(count):
        slot = jnp.int32(0)
        for u in range(t):
            slot = jnp.where(codes[u] == codes[t], u + 1, slot)
        earlier.append(slot)
    latest = {}
    for k in range(parts):
        for c in range(nt * nt):
            slot = jnp.int32(0)
            for t in range(count):
                slot = jnp.where(codes[t] == peers[k] * (nt * nt) + c, t + 1, slot)
            latest[k, c] = slot
    runs[0] = jnp.zeros((tile, tile), F32)
    for load in loads[3:5]:
        load.wait()
    for t in range(count):
        runs[t + 1] = runs[earlier[t]] + adj_ref[t].astype(F32)

    def build(k):
        for c in range(nt * nt):
            rows_here = pl.ds((c // nt) * tile, tile)
            cols_here = pl.ds((c % nt) * tile, tile)
            dense[k, rows_here, cols_here] = runs[latest[k, c]].astype(BF16)

    def forward_copy(k):
        return pltpu.make_async_remote_copy(
            src_ref=fsend.at[k], dst_ref=frecv.at[k], send_sem=fs_sem.at[k], recv_sem=fr_sem.at[k],
            device_id=(peers[k], grp), device_id_type=MESH,
        )

    def gather_copy(k):
        return pltpu.make_async_remote_copy(
            src_ref=gsend, dst_ref=grecv.at[k], send_sem=gs_sem.at[k], recv_sem=gr_sem.at[k],
            device_id=(peers[k], grp), device_id_type=MESH,
        )

    half = nodes // 2
    lower, upper = pl.ds(0, half), pl.ds(half, half)

    def hop(src, dst, i, send, recv, k):
        return pltpu.make_async_remote_copy(
            src_ref=src, dst_ref=dst, send_sem=send.at[i], recv_sem=recv.at[i],
            device_id=(peers[k], grp), device_id_type=MESH,
        )

    relayed = parts == 4
    if relayed:
        forward_hops = [
            hop(fsend.at[3, lower], frecv.at[3, lower], 0, fs_sem, fr_sem, 1),
            hop(fsend.at[3, upper], frecv.at[3, upper], 1, fs_sem, fr_sem, 2),
            hop(fsend.at[1, lower], frecv.at[1, lower], 2, fs_sem, fr_sem, 1),
            hop(fsend.at[2, upper], frecv.at[2, upper], 3, fs_sem, fr_sem, 2),
            hop(fsend.at[1, upper], frecv.at[1, upper], 4, fs_sem, fr_sem, 1),
            hop(fsend.at[2, lower], frecv.at[2, lower], 5, fs_sem, fr_sem, 2),
        ]
        gather_hops = [
            hop(gsend.at[lower], grecv.at[1, lower], 0, gs_sem, gr_sem, 1),
            hop(gsend.at[upper], grecv.at[2, upper], 1, gs_sem, gr_sem, 2),
            hop(gsend.at[upper], grecv.at[1, upper], 2, gs_sem, gr_sem, 1),
            hop(gsend.at[lower], grecv.at[2, lower], 3, gs_sem, gr_sem, 2),
            hop(grecv.at[2, upper], grecv.at[3, upper], 4, gs_sem, gr_sem, 1),
            hop(grecv.at[1, lower], grecv.at[3, lower], 5, gs_sem, gr_sem, 2),
        ]
    else:
        forward_hops = [forward_copy(k) for k in range(1, parts)]
        gather_hops = [gather_copy(k) for k in range(1, parts)]

    x = x_ref[...]
    order = list(range(parts - 1, 0, -1))
    if relayed:
        build(3)
        fsend[3] = dot(dense[3], x).astype(BF16)
        pl.semaphore_wait(barrier, len(partners))
        forward_hops[0].start()
        forward_hops[1].start()
        build(1)
        to_one = dot(dense[1], x)
        fsend[1, :half] = to_one[:half].astype(BF16)
        forward_hops[2].start()
        build(2)
        to_two = dot(dense[2], x)
        fsend[2, half:] = to_two[half:].astype(BF16)
        forward_hops[3].start()
        forward_hops[1].wait_recv()
        fsend[1, half:] = (to_one[half:] + frecv[3, half:].astype(F32)).astype(BF16)
        forward_hops[4].start()
        forward_hops[0].wait_recv()
        fsend[2, :half] = (to_two[:half] + frecv[3, :half].astype(F32)).astype(BF16)
        forward_hops[5].start()
    else:
        for k in order:
            build(k)
            fsend[k] = dot(dense[k], x).astype(BF16)
            if k == order[0]:
                pl.semaphore_wait(barrier, len(partners))
            forward_hops[k - 1].start()
    build(0)
    for load in loads[5:]:
        load.wait()
    agg = dot(dense[0], x)
    pre_self = dot(x, ws_ref[...])
    both_t[0] = x.T
    for k in range(parts):
        dense_t[k] = dense[k].T
    if relayed:
        for copy in forward_hops[2:]:
            copy.wait_recv()
        agg = agg + frecv[1].astype(F32) + frecv[2].astype(F32)
    else:
        for k in order:
            forward_hops[k - 1].wait_recv()
            agg = agg + frecv[k].astype(F32)
    agg_low = agg.astype(BF16)
    both_t[1] = agg_low.T
    pre = pre_self + dot(agg_low, wn_ref[...])
    sig = jax.nn.sigmoid(pre)
    dpre = (og_ref[...].astype(F32) * sig * (1.0 + pre * (1.0 - sig))).astype(BF16)

    def sibling_copy(i, src, dst):
        return pltpu.make_async_remote_copy(
            src_ref=src, dst_ref=dst, send_sem=sib_s.at[i], recv_sem=sib_r.at[i],
            device_id=sibling, device_id_type=MESH,
        )

    halving = sibling_copy(parts, wsend, wsib)
    wsend[...] = dot(both_t[1 - core], dpre).astype(BF16)
    halving.start()
    gsend[...] = dot(dpre, wn_ref[...], 1, 1).astype(BF16)
    own = dot(both_t[core], dpre)

    def scatter_copy(k):
        start = pl.multiple_of(peers[k] * rows, rows)
        return pltpu.make_async_remote_copy(
            src_ref=wsum.at[pl.ds(start, rows)], dst_ref=dslots.at[k], send_sem=rs_s.at[k],
            recv_sem=rs_r.at[k], device_id=(peers[k], grp), device_id_type=MESH,
        )

    def layer_copy(k):
        return pltpu.make_async_remote_copy(
            src_ref=zslots.at[layer], dst_ref=zslots.at[layer], send_sem=z_s.at[k],
            recv_sem=z_r.at[k], device_id=layers[k], device_id_type=MESH,
        )

    mine = pl.ds(pl.multiple_of(dom * rows, rows), rows)

    def spread_copy(k):
        return pltpu.make_async_remote_copy(
            src_ref=wfull.at[core, mine], dst_ref=wfull.at[core, mine], send_sem=ag_s.at[k],
            recv_sem=ag_r.at[k], device_id=(peers[k], grp), device_id_type=MESH,
        )

    halving.wait_recv()
    wsum[...] = (own + wsib[...].astype(F32)).astype(BF16)
    for k in order:
        scatter_copy(k).start()

    out_ref[...] = (pre * sig).astype(BF16)
    stores = [
        pltpu.make_async_copy(out_ref, out_hbm, out_sem.at[0]),
        pltpu.make_async_copy(fg_ref, fg_hbm, out_sem.at[1]),
    ]
    stores[0].start()
    local_sum[...] = dot(dpre, ws_ref[...], 1, 1) + dot(dense_t[0], gsend[...])

    total = wsum[mine, :].astype(F32)
    for k in order:
        scatter_copy(k).wait_recv()
        total = total + dslots[k].astype(F32)
    zslots[layer] = total.astype(BF16)
    for k in range(depth - 1, 0, -1):
        layer_copy(k).start()
    for copy in gather_hops[:4] if relayed else gather_hops:
        copy.start()
    if relayed:
        gather_hops[1].wait_recv()
        gather_hops[4].start()
        gather_hops[0].wait_recv()
        gather_hops[5].start()
    for k in range(1, depth):
        layer_copy(k).wait_recv()
    total = zslots[0].astype(F32)
    for k in range(1, depth):
        total = total + zslots[k].astype(F32)
    wfull[core, mine, :] = (total * scale).astype(BF16)
    for k in order:
        spread_copy(k).start()
    finals = []

    def forward_piece(k):
        piece = wfull.at[core, pl.ds(pl.multiple_of(peers[k] * rows, rows), rows)]
        finals.append(sibling_copy(k, piece, piece))
        finals[-1].start()

    forward_piece(0)
    grad = local_sum[...]
    for copy in gather_hops[2:] if relayed else gather_hops:
        copy.wait_recv()
    for k in range(1, parts):
        grad = grad + dot(dense_t[k], grecv[k])
    fg_ref[...] = grad.astype(BF16)
    stores[1].start()

    for k in order[::-1]:
        spread_copy(k).wait_recv()
        forward_piece(k)
    halves = [
        pltpu.make_async_copy(wg_ref.at[half], wg_hbm.at[half], out_sem.at[2 + i])
        for i, half in enumerate((core, 1 - core))
    ]
    wg_ref[core] = wfull[core].astype(F32)
    halves[0].start()
    for final in finals:
        final.wait_recv()
    wg_ref[1 - core] = wfull[1 - core].astype(F32)
    halves[1].start()
    halving.wait_send()
    for final in finals:
        final.wait_send()
    for k in order:
        scatter_copy(k).wait_send()
        spread_copy(k).wait_send()
    for copy in forward_hops + gather_hops:
        copy.wait_send()
    for k in range(1, depth):
        layer_copy(k).wait_send()
    for store in stores + halves:
        store.wait()


def finish(out_ref, fg_ref, wg_ref, out_hbm, fg_hbm, wg_hbm, out_v, fg_v, wg_v, in_sem, out_sem):
    trips = [
        (wg_ref.at[0], wg_v.at[0], wg_hbm.at[0]),
        (wg_ref.at[1], wg_v.at[1], wg_hbm.at[1]),
        (out_ref, out_v, out_hbm),
        (fg_ref, fg_v, fg_hbm),
    ]
    loads = [pltpu.make_async_copy(a, b, in_sem.at[i]) for i, (a, b, _) in enumerate(trips)]
    stores = [pltpu.make_async_copy(b, c, out_sem.at[i]) for i, (_, b, c) in enumerate(trips)]
    for load in loads:
        load.start()
    for load, store in zip(loads, stores):
        load.wait()
        store.start()
    for store in stores:
        store.wait()


def body(features, adjacency, src_tile, dst_peer, dst_tile, w_self, w_neigh, out_grad):
    nodes, width = features.shape
    count, tile = adjacency.shape[:2]
    parts, groups = lax.axis_size("dom"), lax.axis_size("grp")
    depth = groups // CORES
    scale = 1.0 / math.sqrt(nodes * parts * groups)
    rows = width // parts
    hops = max(parts, 6)
    hbm = pl.BlockSpec(memory_space=pltpu.HBM)
    square = (nodes, width)
    dma = pltpu.SemaphoreType.DMA
    output, feat_grad, grads = pl.pallas_call(
        functools.partial(kernel, parts, depth, scale),
        out_shape=(
            jax.ShapeDtypeStruct(square, BF16),
            jax.ShapeDtypeStruct(square, BF16),
            jax.ShapeDtypeStruct((2, width, width), F32),
        ),
        in_specs=[hbm] * 8,
        out_specs=(hbm, hbm, hbm),
        scratch_shapes=[
            pltpu.SMEM(src_tile.shape, jnp.int32),
            pltpu.SMEM(src_tile.shape, jnp.int32),
            pltpu.SMEM(src_tile.shape, jnp.int32),
            pltpu.VMEM(square, BF16),
            pltpu.VMEM(adjacency.shape, BF16),
            pltpu.VMEM(w_self.shape, BF16),
            pltpu.VMEM(w_neigh.shape, BF16),
            pltpu.VMEM(square, BF16),
            pltpu.VMEM((count + 1, tile, tile), F32),
            pltpu.VMEM((parts, nodes, nodes), BF16),
            pltpu.VMEM((parts, nodes, nodes), BF16),
            pltpu.VMEM((parts,) + square, BF16),
            pltpu.VMEM((parts,) + square, BF16),
            pltpu.VMEM(square, BF16),
            pltpu.VMEM((parts,) + square, BF16),
            pltpu.VMEM((2, width, nodes), BF16),
            pltpu.VMEM((width, width), BF16),
            pltpu.VMEM((width, width), BF16),
            pltpu.VMEM((width, width), BF16),
            pltpu.VMEM((parts, rows, width), BF16),
            pltpu.VMEM((depth, rows, width), BF16),
            pltpu.VMEM((2, width, width), BF16),
            pltpu.VMEM(square, BF16),
            pltpu.VMEM(square, BF16),
            pltpu.VMEM((2, width, width), F32),
            pltpu.VMEM(square, F32),
            dma((8,)), dma((4,)), dma((hops,)), dma((hops,)), dma((hops,)), dma((hops,)),
            dma((parts + 1,)), dma((parts + 1,)), dma((parts,)), dma((parts,)),
            dma((depth,)), dma((depth,)), dma((parts,)), dma((parts,)),
        ],
        compiler_params=pltpu.CompilerParams(
            collective_id=0, has_side_effects=True, vmem_limit_bytes=VMEM_BYTES
        ),
        name="sage_layer",
    )(src_tile, dst_peer[:, 0], dst_tile, features, adjacency, w_self, w_neigh, out_grad)
    return pl.pallas_call(
        finish,
        out_shape=(
            jax.ShapeDtypeStruct(square, BF16),
            jax.ShapeDtypeStruct(square, BF16),
            jax.ShapeDtypeStruct((2, width, width), F32),
        ),
        in_specs=[hbm] * 3,
        out_specs=(hbm, hbm, hbm),
        scratch_shapes=[
            pltpu.VMEM(square, BF16),
            pltpu.VMEM(square, BF16),
            pltpu.VMEM((2, width, width), F32),
            dma((4,)), dma((4,)),
        ],
        compiler_params=pltpu.CompilerParams(vmem_limit_bytes=VMEM_BYTES),
        name="write_results",
    )(output, feat_grad, grads)


def solution(mesh):
    shard = ("dom", "grp")
    in_specs = (
        P(shard, None),
        P(shard, None, None),
        P(shard),
        P(shard, None),
        P(shard),
        P(),
        P(),
        P(shard, None),
    )
    out_specs = (P(shard, None), P(shard, None), P())
    return jax.shard_map(body, mesh=mesh, in_specs=in_specs, out_specs=out_specs, check_vma=False)
```

```python
import functools
import math

import jax
import jax.numpy as jnp
from jax import lax
from jax.experimental import pallas as pl
from jax.experimental.pallas import tpu as pltpu
from jax.sharding import PartitionSpec as P

MESH = pl.DeviceIdType.MESH
BF16 = jnp.bfloat16
F32 = jnp.float32
CORES = 2
VMEM_BYTES = 63 * 1024 * 1024


def dot(a, b, ca=1, cb=0):
    return lax.dot_general(a, b, (((ca,), (cb,)), ((), ())), preferred_element_type=F32)


def flip(index, k, size):
    total, bit = 0, 1
    while bit < size:
        digit = lax.rem(index // bit, 2)
        total = total + bit * ((1 - digit) if (k // bit) % 2 else digit)
        bit *= 2
    return total


def kernel(
    parts, depth, scale,
    src_hbm, peer_hbm, tile_hbm, x_hbm, adj_hbm, ws_hbm, wn_hbm, og_hbm,
    out_hbm, fg_hbm, wg_hbm,
    src_ref, peer_ref, tile_ref, x_ref, adj_ref, ws_ref, wn_ref, og_ref,
    runs, dense, dense_t, fsend, frecv, gsend, grecv, both_t, wsend, wsib, wsum, dslots, zslots, wfull, out_ref, fg_ref, wg_ref, local_sum,
    in_sem, out_sem, fs_sem, fr_sem, gs_sem, gr_sem, sib_s, sib_r, rs_s, rs_r, z_s, z_r, ag_s, ag_r,
):
    dom = lax.axis_index("dom")
    grp = lax.axis_index("grp")
    count, tile = adj_ref.shape[0], adj_ref.shape[1]
    nodes, width = x_ref.shape
    nt = nodes // tile
    core = lax.rem(grp, CORES)
    layer = grp // CORES
    rows = width // parts
    sibling = (dom, layer * CORES + (1 - core))

    loads = [
        pltpu.make_async_copy(hbm, local, in_sem.at[i])
        for i, (hbm, local) in enumerate([
            (peer_hbm, peer_ref), (tile_hbm, tile_ref), (src_hbm, src_ref), (adj_hbm, adj_ref),
            (x_hbm, x_ref), (ws_hbm, ws_ref), (wn_hbm, wn_ref), (og_hbm, og_ref),
        ])
    ]
    for load in loads:
        load.start()

    peers = [flip(dom, k, parts) for k in range(parts)]

    layers = [(dom, flip(layer, k, depth) * CORES + core) for k in range(depth)]

    barrier = pltpu.get_barrier_semaphore()
    partners = [(peers[k], grp) for k in range(1, parts)] + layers[1:] + [sibling]
    for partner in partners:
        pl.semaphore_signal(barrier, inc=1, device_id=partner, device_id_type=MESH)

    for load in loads[:3]:
        load.wait()
    codes = [(peer_ref[t] * nt + tile_ref[t]) * nt + src_ref[t] for t in range(count)]
    earlier = []
    for t in range(count):
        slot = jnp.int32(0)
        for u in range(t):
            slot = jnp.where(codes[u] == codes[t], u + 1, slot)
        earlier.append(slot)
    latest = {}
    for k in range(parts):
        for c in range(nt * nt):
            slot = jnp.int32(0)
            for t in range(count):
                slot = jnp.where(codes[t] == peers[k] * (nt * nt) + c, t + 1, slot)
            latest[k, c] = slot
    runs[0] = jnp.zeros((tile, tile), F32)
    for load in loads[3:5]:
        load.wait()
    for t in range(count):
        runs[t + 1] = runs[earlier[t]] + adj_ref[t].astype(F32)

    def build(k):
        for c in range(nt * nt):
            rows_here = pl.ds((c // nt) * tile, tile)
            cols_here = pl.ds((c % nt) * tile, tile)
            dense[k, rows_here, cols_here] = runs[latest[k, c]].astype(BF16)

    def forward_copy(k):
        return pltpu.make_async_remote_copy(
            src_ref=fsend.at[k], dst_ref=frecv.at[k], send_sem=fs_sem.at[k], recv_sem=fr_sem.at[k],
            device_id=(peers[k], grp), device_id_type=MESH,
        )

    def gather_copy(k):
        return pltpu.make_async_remote_copy(
            src_ref=gsend, dst_ref=grecv.at[k], send_sem=gs_sem.at[k], recv_sem=gr_sem.at[k],
            device_id=(peers[k], grp), device_id_type=MESH,
        )

    x = x_ref[...]
    order = list(range(parts - 1, 0, -1))
    for k in order:
        build(k)
        fsend[k] = dot(dense[k], x).astype(BF16)
        if k == order[0]:
            pl.semaphore_wait(barrier, len(partners))
        forward_copy(k).start()
    build(0)
    for load in loads[5:]:
        load.wait()
    agg = dot(dense[0], x)
    pre_self = dot(x, ws_ref[...])
    both_t[0] = x.T
    for k in range(parts):
        dense_t[k] = dense[k].T
    for k in order[::-1]:
        forward_copy(k).wait_recv()
        agg = agg + frecv[k].astype(F32)
    agg_low = agg.astype(BF16)
    both_t[1] = agg_low.T
    pre = pre_self + dot(agg_low, wn_ref[...])
    sig = jax.nn.sigmoid(pre)
    dpre = (og_ref[...].astype(F32) * sig * (1.0 + pre * (1.0 - sig))).astype(BF16)

    def sibling_copy(i, src, dst):
        return pltpu.make_async_remote_copy(
            src_ref=src, dst_ref=dst, send_sem=sib_s.at[i], recv_sem=sib_r.at[i],
            device_id=sibling, device_id_type=MESH,
        )

    halving = sibling_copy(parts, wsend, wsib)
    wsend[...] = dot(both_t[1 - core], dpre).astype(BF16)
    halving.start()
    gsend[...] = dot(dpre, wn_ref[...], 1, 1).astype(BF16)
    for k in order:
        gather_copy(k).start()
    own = dot(both_t[core], dpre)

    def scatter_copy(k):
        start = pl.multiple_of(peers[k] * rows, rows)
        return pltpu.make_async_remote_copy(
            src_ref=wsum.at[pl.ds(start, rows)], dst_ref=dslots.at[k], send_sem=rs_s.at[k],
            recv_sem=rs_r.at[k], device_id=(peers[k], grp), device_id_type=MESH,
        )

    def layer_copy(k):
        return pltpu.make_async_remote_copy(
            src_ref=zslots.at[layer], dst_ref=zslots.at[layer], send_sem=z_s.at[k],
            recv_sem=z_r.at[k], device_id=layers[k], device_id_type=MESH,
        )

    mine = pl.ds(pl.multiple_of(dom * rows, rows), rows)

    def spread_copy(k):
        return pltpu.make_async_remote_copy(
            src_ref=wfull.at[core, mine], dst_ref=wfull.at[core, mine], send_sem=ag_s.at[k],
            recv_sem=ag_r.at[k], device_id=(peers[k], grp), device_id_type=MESH,
        )

    halving.wait_recv()
    wsum[...] = (own + wsib[...].astype(F32)).astype(BF16)
    for k in order:
        scatter_copy(k).start()

    out_ref[...] = (pre * sig).astype(BF16)
    stores = [
        pltpu.make_async_copy(out_ref, out_hbm, out_sem.at[0]),
        pltpu.make_async_copy(fg_ref, fg_hbm, out_sem.at[1]),
    ]
    stores[0].start()
    local_sum[...] = dot(dpre, ws_ref[...], 1, 1) + dot(dense_t[0], gsend[...])

    total = wsum[mine, :].astype(F32)
    for k in order:
        scatter_copy(k).wait_recv()
        total = total + dslots[k].astype(F32)
    zslots[layer] = total.astype(BF16)
    for k in range(depth - 1, 0, -1):
        layer_copy(k).start()
    for k in range(1, depth):
        layer_copy(k).wait_recv()
    total = zslots[0].astype(F32)
    for k in range(1, depth):
        total = total + zslots[k].astype(F32)
    wfull[core, mine, :] = (total * scale).astype(BF16)
    for k in order:
        spread_copy(k).start()
    finals = []

    def forward_piece(k):
        piece = wfull.at[core, pl.ds(pl.multiple_of(peers[k] * rows, rows), rows)]
        finals.append(sibling_copy(k, piece, piece))
        finals[-1].start()

    forward_piece(0)
    grad = local_sum[...]
    for k in range(1, parts):
        gather_copy(k).wait_recv()
        grad = grad + dot(dense_t[k], grecv[k])
    fg_ref[...] = grad.astype(BF16)
    stores[1].start()

    for k in order[::-1]:
        spread_copy(k).wait_recv()
        forward_piece(k)
    halves = [
        pltpu.make_async_copy(wg_ref.at[half], wg_hbm.at[half], out_sem.at[2 + i])
        for i, half in enumerate((core, 1 - core))
    ]
    wg_ref[core] = wfull[core].astype(F32)
    halves[0].start()
    for final in finals:
        final.wait_recv()
    wg_ref[1 - core] = wfull[1 - core].astype(F32)
    halves[1].start()
    halving.wait_send()
    for final in finals:
        final.wait_send()
    for k in order:
        scatter_copy(k).wait_send()
        spread_copy(k).wait_send()
    for k in order:
        forward_copy(k).wait_send()
        gather_copy(k).wait_send()
    for k in range(1, depth):
        layer_copy(k).wait_send()
    for store in stores + halves:
        store.wait()


def finish(out_ref, fg_ref, wg_ref, out_hbm, fg_hbm, wg_hbm, out_v, fg_v, wg_v, in_sem, out_sem):
    trips = [
        (wg_ref.at[0], wg_v.at[0], wg_hbm.at[0]),
        (wg_ref.at[1], wg_v.at[1], wg_hbm.at[1]),
        (out_ref, out_v, out_hbm),
        (fg_ref, fg_v, fg_hbm),
    ]
    loads = [pltpu.make_async_copy(a, b, in_sem.at[i]) for i, (a, b, _) in enumerate(trips)]
    stores = [pltpu.make_async_copy(b, c, out_sem.at[i]) for i, (_, b, c) in enumerate(trips)]
    for load in loads:
        load.start()
    for load, store in zip(loads, stores):
        load.wait()
        store.start()
    for store in stores:
        store.wait()


def body(features, adjacency, src_tile, dst_peer, dst_tile, w_self, w_neigh, out_grad):
    nodes, width = features.shape
    count, tile = adjacency.shape[:2]
    parts, groups = lax.axis_size("dom"), lax.axis_size("grp")
    depth = groups // CORES
    scale = 1.0 / math.sqrt(nodes * parts * groups)
    rows = width // parts
    hbm = pl.BlockSpec(memory_space=pltpu.HBM)
    square = (nodes, width)
    dma = pltpu.SemaphoreType.DMA
    output, feat_grad, grads = pl.pallas_call(
        functools.partial(kernel, parts, depth, scale),
        out_shape=(
            jax.ShapeDtypeStruct(square, BF16),
            jax.ShapeDtypeStruct(square, BF16),
            jax.ShapeDtypeStruct((2, width, width), F32),
        ),
        in_specs=[hbm] * 8,
        out_specs=(hbm, hbm, hbm),
        scratch_shapes=[
            pltpu.SMEM(src_tile.shape, jnp.int32),
            pltpu.SMEM(src_tile.shape, jnp.int32),
            pltpu.SMEM(src_tile.shape, jnp.int32),
            pltpu.VMEM(square, BF16),
            pltpu.VMEM(adjacency.shape, BF16),
            pltpu.VMEM(w_self.shape, BF16),
            pltpu.VMEM(w_neigh.shape, BF16),
            pltpu.VMEM(square, BF16),
            pltpu.VMEM((count + 1, tile, tile), F32),
            pltpu.VMEM((parts, nodes, nodes), BF16),
            pltpu.VMEM((parts, nodes, nodes), BF16),
            pltpu.VMEM((parts,) + square, BF16),
            pltpu.VMEM((parts,) + square, BF16),
            pltpu.VMEM(square, BF16),
            pltpu.VMEM((parts,) + square, BF16),
            pltpu.VMEM((2, width, nodes), BF16),
            pltpu.VMEM((width, width), BF16),
            pltpu.VMEM((width, width), BF16),
            pltpu.VMEM((width, width), BF16),
            pltpu.VMEM((parts, rows, width), BF16),
            pltpu.VMEM((depth, rows, width), BF16),
            pltpu.VMEM((2, width, width), BF16),
            pltpu.VMEM(square, BF16),
            pltpu.VMEM(square, BF16),
            pltpu.VMEM((2, width, width), F32),
            pltpu.VMEM(square, F32),
            dma((8,)), dma((4,)), dma((parts,)), dma((parts,)), dma((parts,)), dma((parts,)),
            dma((parts + 1,)), dma((parts + 1,)), dma((parts,)), dma((parts,)),
            dma((depth,)), dma((depth,)), dma((parts,)), dma((parts,)),
        ],
        compiler_params=pltpu.CompilerParams(
            collective_id=0, has_side_effects=True, vmem_limit_bytes=VMEM_BYTES
        ),
        name="sage_layer",
    )(src_tile, dst_peer[:, 0], dst_tile, features, adjacency, w_self, w_neigh, out_grad)
    return pl.pallas_call(
        finish,
        out_shape=(
            jax.ShapeDtypeStruct(square, BF16),
            jax.ShapeDtypeStruct(square, BF16),
            jax.ShapeDtypeStruct((2, width, width), F32),
        ),
        in_specs=[hbm] * 3,
        out_specs=(hbm, hbm, hbm),
        scratch_shapes=[
            pltpu.VMEM(square, BF16),
            pltpu.VMEM(square, BF16),
            pltpu.VMEM((2, width, width), F32),
            dma((4,)), dma((4,)),
        ],
        compiler_params=pltpu.CompilerParams(vmem_limit_bytes=VMEM_BYTES),
        name="write_results",
    )(output, feat_grad, grads)


def solution(mesh):
    shard = ("dom", "grp")
    in_specs = (
        P(shard, None),
        P(shard, None, None),
        P(shard),
        P(shard, None),
        P(shard),
        P(),
        P(),
        P(shard, None),
    )
    out_specs = (P(shard, None), P(shard, None), P())
    return jax.shard_map(body, mesh=mesh, in_specs=in_specs, out_specs=out_specs, check_vma=False)
```

```python
import functools
import math

import jax
import jax.numpy as jnp
from jax import lax
from jax.experimental import pallas as pl
from jax.experimental.pallas import tpu as pltpu
from jax.sharding import PartitionSpec as P

MESH = pl.DeviceIdType.MESH
BF16 = jnp.bfloat16
F32 = jnp.float32
CORES = 2
VMEM_BYTES = 63 * 1024 * 1024


def dot(a, b, ca=1, cb=0):
    return lax.dot_general(a, b, (((ca,), (cb,)), ((), ())), preferred_element_type=F32)


def flip(index, k, size):
    total, bit = 0, 1
    while bit < size:
        digit = lax.rem(index // bit, 2)
        total = total + bit * ((1 - digit) if (k // bit) % 2 else digit)
        bit *= 2
    return total


def kernel(
    parts, depth, scale,
    src_hbm, peer_hbm, tile_hbm, x_hbm, adj_hbm, ws_hbm, wn_hbm, og_hbm,
    out_hbm, fg_hbm, wg_hbm,
    src_ref, peer_ref, tile_ref, x_ref, adj_ref, ws_ref, wn_ref, og_ref,
    runs, dense, dense_t, fsend, frecv, gsend, grecv, both_t, wsend, wsib, wsum, dslots, zslots, wfull, out_ref, fg_ref, wg_ref, local_sum,
    in_sem, out_sem, fs_sem, fr_sem, gs_sem, gr_sem, sib_s, sib_r, rs_s, rs_r, z_s, z_r, ag_s, ag_r,
):
    dom = lax.axis_index("dom")
    grp = lax.axis_index("grp")
    count, tile = adj_ref.shape[0], adj_ref.shape[1]
    nodes, width = x_ref.shape
    nt = nodes // tile
    core = lax.rem(grp, CORES)
    layer = grp // CORES
    rows = width // parts
    sibling = (dom, layer * CORES + (1 - core))

    loads = [
        pltpu.make_async_copy(hbm, local, in_sem.at[i])
        for i, (hbm, local) in enumerate([
            (peer_hbm, peer_ref), (tile_hbm, tile_ref), (src_hbm, src_ref), (adj_hbm, adj_ref),
            (x_hbm, x_ref), (ws_hbm, ws_ref), (wn_hbm, wn_ref), (og_hbm, og_ref),
        ])
    ]
    for load in loads:
        load.start()

    peers = [flip(dom, k, parts) for k in range(parts)]

    layers = [(dom, flip(layer, k, depth) * CORES + core) for k in range(depth)]

    barrier = pltpu.get_barrier_semaphore()
    partners = [(peers[k], grp) for k in range(1, parts)] + layers[1:] + [sibling]
    for partner in partners:
        pl.semaphore_signal(barrier, inc=1, device_id=partner, device_id_type=MESH)

    for load in loads[:3]:
        load.wait()
    codes = [(peer_ref[t] * nt + tile_ref[t]) * nt + src_ref[t] for t in range(count)]
    earlier = []
    for t in range(count):
        slot = jnp.int32(0)
        for u in range(t):
            slot = jnp.where(codes[u] == codes[t], u + 1, slot)
        earlier.append(slot)
    latest = {}
    for k in range(parts):
        for c in range(nt * nt):
            slot = jnp.int32(0)
            for t in range(count):
                slot = jnp.where(codes[t] == peers[k] * (nt * nt) + c, t + 1, slot)
            latest[k, c] = slot
    runs[0] = jnp.zeros((tile, tile), F32)
    for load in loads[3:5]:
        load.wait()
    for t in range(count):
        runs[t + 1] = runs[earlier[t]] + adj_ref[t].astype(F32)

    def build(k):
        for c in range(nt * nt):
            rows_here = pl.ds((c // nt) * tile, tile)
            cols_here = pl.ds((c % nt) * tile, tile)
            dense[k, rows_here, cols_here] = runs[latest[k, c]].astype(BF16)

    def forward_copy(k):
        return pltpu.make_async_remote_copy(
            src_ref=fsend.at[k], dst_ref=frecv.at[k], send_sem=fs_sem.at[k], recv_sem=fr_sem.at[k],
            device_id=(peers[k], grp), device_id_type=MESH,
        )

    def gather_copy(k):
        return pltpu.make_async_remote_copy(
            src_ref=gsend, dst_ref=grecv.at[k], send_sem=gs_sem.at[k], recv_sem=gr_sem.at[k],
            device_id=(peers[k], grp), device_id_type=MESH,
        )

    half = nodes // 2
    lower, upper = pl.ds(0, half), pl.ds(half, half)

    def hop(src, dst, i, send, recv, k):
        return pltpu.make_async_remote_copy(
            src_ref=src, dst_ref=dst, send_sem=send.at[i], recv_sem=recv.at[i],
            device_id=(peers[k], grp), device_id_type=MESH,
        )

    relayed = parts == 4
    if relayed:
        forward_hops = [
            hop(fsend.at[3, lower], frecv.at[3, lower], 0, fs_sem, fr_sem, 1),
            hop(fsend.at[3, upper], frecv.at[3, upper], 1, fs_sem, fr_sem, 2),
            hop(fsend.at[1, lower], frecv.at[1, lower], 2, fs_sem, fr_sem, 1),
            hop(fsend.at[2, upper], frecv.at[2, upper], 3, fs_sem, fr_sem, 2),
            hop(fsend.at[1, upper], frecv.at[1, upper], 4, fs_sem, fr_sem, 1),
            hop(fsend.at[2, lower], frecv.at[2, lower], 5, fs_sem, fr_sem, 2),
        ]
        gather_hops = [
            hop(gsend.at[lower], grecv.at[1, lower], 0, gs_sem, gr_sem, 1),
            hop(gsend.at[upper], grecv.at[2, upper], 1, gs_sem, gr_sem, 2),
            hop(gsend.at[upper], grecv.at[1, upper], 2, gs_sem, gr_sem, 1),
            hop(gsend.at[lower], grecv.at[2, lower], 3, gs_sem, gr_sem, 2),
            hop(grecv.at[2, upper], grecv.at[3, upper], 4, gs_sem, gr_sem, 1),
            hop(grecv.at[1, lower], grecv.at[3, lower], 5, gs_sem, gr_sem, 2),
        ]
    else:
        forward_hops = [forward_copy(k) for k in range(1, parts)]
        gather_hops = [gather_copy(k) for k in range(1, parts)]

    x = x_ref[...]
    order = list(range(parts - 1, 0, -1))
    if relayed:
        build(3)
        fsend[3] = dot(dense[3], x).astype(BF16)
        pl.semaphore_wait(barrier, len(partners))
        forward_hops[0].start()
        forward_hops[1].start()
        build(1)
        to_one = dot(dense[1], x)
        fsend[1, :half] = to_one[:half].astype(BF16)
        forward_hops[2].start()
        build(2)
        to_two = dot(dense[2], x)
        fsend[2, half:] = to_two[half:].astype(BF16)
        forward_hops[3].start()
        forward_hops[1].wait_recv()
        fsend[1, half:] = (to_one[half:] + frecv[3, half:].astype(F32)).astype(BF16)
        forward_hops[4].start()
        forward_hops[0].wait_recv()
        fsend[2, :half] = (to_two[:half] + frecv[3, :half].astype(F32)).astype(BF16)
        forward_hops[5].start()
    else:
        for k in order:
            build(k)
            fsend[k] = dot(dense[k], x).astype(BF16)
            if k == order[0]:
                pl.semaphore_wait(barrier, len(partners))
            forward_hops[k - 1].start()
    build(0)
    for load in loads[5:]:
        load.wait()
    agg = dot(dense[0], x)
    pre_self = dot(x, ws_ref[...])
    both_t[0] = x.T
    for k in range(parts):
        dense_t[k] = dense[k].T
    if relayed:
        for copy in forward_hops[2:]:
            copy.wait_recv()
        agg = agg + frecv[1].astype(F32) + frecv[2].astype(F32)
    else:
        for k in order:
            forward_hops[k - 1].wait_recv()
            agg = agg + frecv[k].astype(F32)
    agg_low = agg.astype(BF16)
    both_t[1] = agg_low.T
    pre = pre_self + dot(agg_low, wn_ref[...])
    sig = jax.nn.sigmoid(pre)
    dpre = (og_ref[...].astype(F32) * sig * (1.0 + pre * (1.0 - sig))).astype(BF16)

    def sibling_copy(i, src, dst):
        return pltpu.make_async_remote_copy(
            src_ref=src, dst_ref=dst, send_sem=sib_s.at[i], recv_sem=sib_r.at[i],
            device_id=sibling, device_id_type=MESH,
        )

    halving = sibling_copy(parts, wsend, wsib)
    wsend[...] = dot(both_t[1 - core], dpre).astype(BF16)
    halving.start()
    gsend[...] = dot(dpre, wn_ref[...], 1, 1).astype(BF16)
    own = dot(both_t[core], dpre)

    def scatter_copy(k):
        start = pl.multiple_of(peers[k] * rows, rows)
        return pltpu.make_async_remote_copy(
            src_ref=wsum.at[pl.ds(start, rows)], dst_ref=dslots.at[k], send_sem=rs_s.at[k],
            recv_sem=rs_r.at[k], device_id=(peers[k], grp), device_id_type=MESH,
        )

    pieces = 2 if rows % 32 == 0 else 1
    part = rows // pieces

    def layer_copy(k, p):
        place = zslots.at[layer, pl.ds(p * part, part)]
        return pltpu.make_async_remote_copy(
            src_ref=place, dst_ref=place, send_sem=z_s.at[p * depth + k],
            recv_sem=z_r.at[p * depth + k], device_id=layers[k], device_id_type=MESH,
        )

    mine = pl.ds(pl.multiple_of(dom * rows, rows), rows)

    def own_part(p):
        return pl.ds(pl.multiple_of(dom * rows + p * part, part), part)

    def spread_copy(k, p):
        place = wfull.at[core, own_part(p)]
        return pltpu.make_async_remote_copy(
            src_ref=place, dst_ref=place, send_sem=ag_s.at[p * parts + k],
            recv_sem=ag_r.at[p * parts + k], device_id=(peers[k], grp), device_id_type=MESH,
        )

    halving.wait_recv()
    wsum[...] = (own + wsib[...].astype(F32)).astype(BF16)
    for k in order:
        scatter_copy(k).start()
    for copy in gather_hops[:4] if relayed else gather_hops:
        copy.start()

    out_ref[...] = (pre * sig).astype(BF16)
    stores = [
        pltpu.make_async_copy(out_ref, out_hbm, out_sem.at[0]),
        pltpu.make_async_copy(fg_ref, fg_hbm, out_sem.at[1]),
    ]
    stores[0].start()
    local_sum[...] = dot(dpre, ws_ref[...], 1, 1) + dot(dense_t[0], gsend[...])

    total = wsum[mine, :].astype(F32)
    for k in order:
        scatter_copy(k).wait_recv()
        total = total + dslots[k].astype(F32)
    zslots[layer] = total.astype(BF16)
    for p in range(pieces):
        for k in range(depth - 1, 0, -1):
            layer_copy(k, p).start()
    if relayed:
        gather_hops[1].wait_recv()
        gather_hops[4].start()
        gather_hops[0].wait_recv()
        gather_hops[5].start()
    for p in range(pieces):
        for k in range(1, depth):
            layer_copy(k, p).wait_recv()
        here = pl.ds(p * part, part)
        total = zslots[0, here].astype(F32)
        for k in range(1, depth):
            total = total + zslots[k, here].astype(F32)
        wfull[core, own_part(p), :] = (total * scale).astype(BF16)
        for k in order:
            spread_copy(k, p).start()
    finals = []

    def forward_piece(k):
        piece = wfull.at[core, pl.ds(pl.multiple_of(peers[k] * rows, rows), rows)]
        finals.append(sibling_copy(k, piece, piece))
        finals[-1].start()

    forward_piece(0)
    grad = local_sum[...]
    for copy in gather_hops[2:] if relayed else gather_hops:
        copy.wait_recv()
    for k in range(1, parts):
        grad = grad + dot(dense_t[k], grecv[k])
    fg_ref[...] = grad.astype(BF16)
    stores[1].start()

    for k in order[::-1]:
        for p in range(pieces):
            spread_copy(k, p).wait_recv()
        forward_piece(k)
    halves = [
        pltpu.make_async_copy(wg_ref.at[half], wg_hbm.at[half], out_sem.at[2 + i])
        for i, half in enumerate((core, 1 - core))
    ]
    wg_ref[core] = wfull[core].astype(F32)
    halves[0].start()
    for final in finals:
        final.wait_recv()
    wg_ref[1 - core] = wfull[1 - core].astype(F32)
    halves[1].start()
    halving.wait_send()
    for final in finals:
        final.wait_send()
    for k in order:
        scatter_copy(k).wait_send()
        for p in range(pieces):
            spread_copy(k, p).wait_send()
    for copy in forward_hops + gather_hops:
        copy.wait_send()
    for k in range(1, depth):
        for p in range(pieces):
            layer_copy(k, p).wait_send()
    for store in stores + halves:
        store.wait()


def finish(out_ref, fg_ref, wg_ref, out_hbm, fg_hbm, wg_hbm, out_v, fg_v, wg_v, in_sem, out_sem):
    trips = [
        (wg_ref.at[0], wg_v.at[0], wg_hbm.at[0]),
        (wg_ref.at[1], wg_v.at[1], wg_hbm.at[1]),
        (out_ref, out_v, out_hbm),
        (fg_ref, fg_v, fg_hbm),
    ]
    loads = [pltpu.make_async_copy(a, b, in_sem.at[i]) for i, (a, b, _) in enumerate(trips)]
    stores = [pltpu.make_async_copy(b, c, out_sem.at[i]) for i, (_, b, c) in enumerate(trips)]
    for load in loads:
        load.start()
    for load, store in zip(loads, stores):
        load.wait()
        store.start()
    for store in stores:
        store.wait()


def body(features, adjacency, src_tile, dst_peer, dst_tile, w_self, w_neigh, out_grad):
    nodes, width = features.shape
    count, tile = adjacency.shape[:2]
    parts, groups = lax.axis_size("dom"), lax.axis_size("grp")
    depth = groups // CORES
    scale = 1.0 / math.sqrt(nodes * parts * groups)
    rows = width // parts
    hops = max(parts, 6)
    hbm = pl.BlockSpec(memory_space=pltpu.HBM)
    square = (nodes, width)
    dma = pltpu.SemaphoreType.DMA
    output, feat_grad, grads = pl.pallas_call(
        functools.partial(kernel, parts, depth, scale),
        out_shape=(
            jax.ShapeDtypeStruct(square, BF16),
            jax.ShapeDtypeStruct(square, BF16),
            jax.ShapeDtypeStruct((2, width, width), F32),
        ),
        in_specs=[hbm] * 8,
        out_specs=(hbm, hbm, hbm),
        scratch_shapes=[
            pltpu.SMEM(src_tile.shape, jnp.int32),
            pltpu.SMEM(src_tile.shape, jnp.int32),
            pltpu.SMEM(src_tile.shape, jnp.int32),
            pltpu.VMEM(square, BF16),
            pltpu.VMEM(adjacency.shape, BF16),
            pltpu.VMEM(w_self.shape, BF16),
            pltpu.VMEM(w_neigh.shape, BF16),
            pltpu.VMEM(square, BF16),
            pltpu.VMEM((count + 1, tile, tile), F32),
            pltpu.VMEM((parts, nodes, nodes), BF16),
            pltpu.VMEM((parts, nodes, nodes), BF16),
            pltpu.VMEM((parts,) + square, BF16),
            pltpu.VMEM((parts,) + square, BF16),
            pltpu.VMEM(square, BF16),
            pltpu.VMEM((parts,) + square, BF16),
            pltpu.VMEM((2, width, nodes), BF16),
            pltpu.VMEM((width, width), BF16),
            pltpu.VMEM((width, width), BF16),
            pltpu.VMEM((width, width), BF16),
            pltpu.VMEM((parts, rows, width), BF16),
            pltpu.VMEM((depth, rows, width), BF16),
            pltpu.VMEM((2, width, width), BF16),
            pltpu.VMEM(square, BF16),
            pltpu.VMEM(square, BF16),
            pltpu.VMEM((2, width, width), F32),
            pltpu.VMEM(square, F32),
            dma((8,)), dma((4,)), dma((hops,)), dma((hops,)), dma((hops,)), dma((hops,)),
            dma((parts + 1,)), dma((parts + 1,)), dma((parts,)), dma((parts,)),
            dma((2 * depth,)), dma((2 * depth,)), dma((2 * parts,)), dma((2 * parts,)),
        ],
        compiler_params=pltpu.CompilerParams(
            collective_id=0, has_side_effects=True, vmem_limit_bytes=VMEM_BYTES
        ),
        name="sage_layer",
    )(src_tile, dst_peer[:, 0], dst_tile, features, adjacency, w_self, w_neigh, out_grad)
    return pl.pallas_call(
        finish,
        out_shape=(
            jax.ShapeDtypeStruct(square, BF16),
            jax.ShapeDtypeStruct(square, BF16),
            jax.ShapeDtypeStruct((2, width, width), F32),
        ),
        in_specs=[hbm] * 3,
        out_specs=(hbm, hbm, hbm),
        scratch_shapes=[
            pltpu.VMEM(square, BF16),
            pltpu.VMEM(square, BF16),
            pltpu.VMEM((2, width, width), F32),
            dma((4,)), dma((4,)),
        ],
        compiler_params=pltpu.CompilerParams(vmem_limit_bytes=VMEM_BYTES),
        name="write_results",
    )(output, feat_grad, grads)


def solution(mesh):
    shard = ("dom", "grp")
    in_specs = (
        P(shard, None),
        P(shard, None, None),
        P(shard),
        P(shard, None),
        P(shard),
        P(),
        P(),
        P(shard, None),
    )
    out_specs = (P(shard, None), P(shard, None), P())
    return jax.shard_map(body, mesh=mesh, in_specs=in_specs, out_specs=out_specs, check_vma=False)
```
